32 devices in a mesh: parts: 2 (over y), tensor: 4 (over z), dp: 4 (over x, core).
Axes of the slice: x: 2, y: 2, z: 4, core: 2. Of those that a mesh axis runs over, the one named last changes fastest.
Arguments:
- attention_output: bfloat16 [8192, 8192], P(('parts', 'dp'), 'tensor'), parts along dimension 0, may hold values from -6 to 6
- projection_output_gradient: bfloat16 [8192, 5120], P(('parts', 'dp'), 'tensor'), parts along dimension 0, may hold values from -6 to 6
- token_adapter_index: int32 [8192], P(('parts', 'dp')), parts along dimension 0, may hold values from 0 to 63
- owner_slot_adapter: int32 [64], replicated, may hold values from 0 to 63, each once
- output_projection_weight: bfloat16 [8192, 5120], P('tensor'), may hold values from -0.0625 to 0.0625
- adapter_down_weight: bfloat16 [64, 16, 8192], P(None, None, 'tensor'), may hold values from -0.0625 to 0.0625
- adapter_up_weight: bfloat16 [64, 16, 5120], P(None, None, 'tensor'), may hold values from -0.078125 to 0.078125
Outputs:
- attention_gradient: bfloat16 [8192, 8192], P(('parts', 'dp'), 'tensor'), parts along dimension 0
- grad_a: float32 [128, 16, 8192], P(('parts', 'dp'), None, 'tensor'), parts along dimension 0
- grad_b: float32 [128, 16, 5120], P(('parts', 'dp'), None, 'tensor'), parts along dimension 0
The draws below stay inside these ranges and needn't reach their ends.
There are 2 independent parts, one for each index of `parts`. The reference program is written for one: setup_inputs(seed, part) draws one part's arguments, and reference() takes and returns one part's arrays. A program takes and returns all parts, laid end to end along the dimension named above; an argument that names none is the same for every part. Nothing has to cross between parts.
Inputs may be any that keep to these rules, and one draw needn't show every extreme that they name: `owner_slot_adapter`: each adapter appears exactly once.
All inputs are finite; a program needn't handle non-finite values.
Results may differ from the reference program's by a relative error of at most 0.0031.
Values may be sent and summed in bfloat16 or wider, within the bound.
No kernel may reach another device: no remote copies, remote signals or barrier semaphores. Data moves between devices by JAX's collectives and lax.ppermute only.
A program may use at most 192 MiB of HBM per device.

```python
import math
import jax
import jax.numpy as jnp
import numpy as np
from jax import lax

MODEL_WIDTH = 5120
ADAPTER_COUNT = 64
ADAPTER_RANK = 16
ATTENTION_WIDTH = 8192
TOKENS = 4096


def plant(entries, own_key, low, high):
    shape = entries.shape
    spot = [jax.random.randint(jax.random.fold_in(own_key, axis), (), 0, shape[axis]) for axis in range(len(shape))]
    entries = entries.at[tuple(spot)].set(low)
    longest = shape.index(max(shape))
    spot[longest] = (spot[longest] + 1) % shape[longest]
    return entries.at[tuple(spot)].set(high)


def shard_levels(own_key, shape, pieces, smallest, high):
    level, own = 1.0, jax.random.fold_in(own_key, 6)
    for axis_at, blocks in pieces:
        heights = jnp.exp(jax.random.uniform(jax.random.fold_in(own, axis_at), (blocks,), jnp.float32, smallest / len(pieces), high / len(pieces)))
        level = level * jnp.repeat(heights, shape[axis_at] // blocks).reshape([-1 if axis == axis_at else 1 for axis in range(len(shape))])
    return level


def cumulative_ranks(amount, lean):
    portions = [(1 << 20) // math.isqrt(grade ** lean) + 1 for grade in range(1, amount + 1)]
    scale = 1 + sum(portions) // (1 << 30)
    return np.cumsum(np.array([max(1, weight // scale) for weight in portions]))


def ranked_ids(key, dims, count, lean):
    grid = cumulative_ranks(count, lean)
    ticket = jax.random.randint(jax.random.fold_in(key, 1), dims, 0, int(grid[count - 1]))
    grade = jnp.searchsorted(jnp.asarray(grid, jnp.int32), ticket, side="right")
    return jax.random.permutation(jax.random.fold_in(key, 2), count)[grade].astype(jnp.int32)


def noise(key, dims, scale, bound, pieces=(), kind=jnp.bfloat16):
    drawn = jax.random.normal(key, dims, jnp.float32) * scale
    if len(pieces) > 0:
        drawn = shard_levels(key, dims, pieces, -0.22, 0.18) * drawn
    return jnp.clip(drawn, min=-bound, max=bound).astype(kind)


def setup_inputs(seed: int = 0, part: int = 0) -> dict:
    key_of = jax.random.split(jax.random.key(seed), 8)
    own_keys = jax.random.split(jax.random.fold_in(key_of[7], part), 8)
    attention_output = noise(own_keys[0], (TOKENS, ATTENTION_WIDTH), 1.0, 6.0, ((0, 4), (1, 4)))
    projection_output_gradient = noise(own_keys[1], (TOKENS, MODEL_WIDTH), 1.0, 6.0, ((0, 4), (1, 4)))
    token_adapter_index = plant(ranked_ids(own_keys[2], (TOKENS,), ADAPTER_COUNT, 2), jax.random.fold_in(own_keys[2], 3), 0, ADAPTER_COUNT - 1).astype(jnp.int32)
    owner_slot_adapter = jax.random.permutation(key_of[3], ADAPTER_COUNT).astype(jnp.int32)
    output_projection_weight = noise(key_of[4], (ATTENTION_WIDTH, MODEL_WIDTH), ATTENTION_WIDTH ** -0.5, 0.0625, ((0, 4),))
    adapter_down_weight = noise(key_of[5], (ADAPTER_COUNT, ADAPTER_RANK, ATTENTION_WIDTH), ATTENTION_WIDTH ** -0.5, 0.0625, ((2, 4),))
    adapter_up_weight = noise(key_of[6], (ADAPTER_COUNT, ADAPTER_RANK, MODEL_WIDTH), MODEL_WIDTH ** -0.5, 0.078125, ((2, 4),))
    return {"attention_output": attention_output, "projection_output_gradient": projection_output_gradient, "token_adapter_index": token_adapter_index, "owner_slot_adapter": owner_slot_adapter, "output_projection_weight": output_projection_weight, "adapter_down_weight": adapter_down_weight, "adapter_up_weight": adapter_up_weight}


ADAPTER_SCALE = 2.0
OBJECTIVE_WEIGHT = 0.05


def pick_rows(selected, values):
    no_value = jnp.zeros((), values.dtype)
    return jnp.where(selected[:, :, None], values[:, None, :], no_value)


def reference(attention_output, projection_output_gradient, token_adapter_index, owner_slot_adapter, output_projection_weight, adapter_down_weight, adapter_up_weight):
    adapter_list, rank_extent, attention_columns = adapter_down_weight.shape
    width_columns = adapter_up_weight.shape[2]
    row_count = attention_output.shape[0]
    row_dims = (((1,), (1,)), ((), ()))
    tok_dims = (((0,), (0,)), ((), ()))
    labels = jnp.arange(adapter_list, dtype=jnp.int32)
    chosen = token_adapter_index[:, None] == labels[None, :]
    input_rows = adapter_down_weight.reshape(adapter_list * rank_extent, attention_columns)
    output_rows = adapter_up_weight.reshape(adapter_list * rank_extent, width_columns)
    u_terms = lax.dot_general(attention_output, input_rows, row_dims, preferred_element_type=jnp.float32)
    u_terms = u_terms.reshape(row_count, adapter_list, rank_extent)
    low_in = jnp.sum(jnp.where(chosen[:, :, None], u_terms, jnp.zeros((), jnp.float32)), axis=1)
    g_terms = lax.dot_general(projection_output_gradient, output_rows, row_dims, preferred_element_type=jnp.float32)
    g_terms = g_terms.reshape(row_count, adapter_list, rank_extent)
    low_out = jnp.sum(jnp.where(chosen[:, :, None], g_terms, jnp.zeros((), jnp.float32)), axis=1)
    in_bf = low_in.astype(jnp.bfloat16)
    out_bf = low_out.astype(jnp.bfloat16)
    g_wide = pick_rows(chosen, out_bf).reshape(row_count, adapter_list * rank_extent)
    adapter_contribution = jnp.dot(g_wide, input_rows, preferred_element_type=jnp.float32)
    frozen_contribution = lax.dot_general(projection_output_gradient, output_projection_weight, row_dims, preferred_element_type=jnp.float32)
    attention_gradient = (frozen_contribution + ADAPTER_SCALE * adapter_contribution).astype(jnp.bfloat16)
    owned_hot = token_adapter_index[:, None] == owner_slot_adapter[None, :]
    g_own = pick_rows(owned_hot, out_bf).reshape(row_count, adapter_list * rank_extent)
    u_own = pick_rows(owned_hot, in_bf).reshape(row_count, adapter_list * rank_extent)
    gradient_multiplier = ADAPTER_SCALE * OBJECTIVE_WEIGHT
    grad_a = gradient_multiplier * lax.dot_general(g_own, attention_output, tok_dims, preferred_element_type=jnp.float32)
    grad_b = gradient_multiplier * lax.dot_general(u_own, projection_output_gradient, tok_dims, preferred_element_type=jnp.float32)
    return attention_gradient, grad_a.reshape(adapter_list, rank_extent, attention_columns), grad_b.reshape(adapter_list, rank_extent, width_columns)
```

```python
import jax
import jax.numpy as jnp
from jax import lax
from jax.sharding import PartitionSpec as P

ADAPTER_SCALE = 2.0
OBJECTIVE_WEIGHT = 0.05


def pairs(size, distance):
    return [(i, i ^ distance) for i in range(size)]


def power_of_two(size):
    return size & (size - 1) == 0


def low_rank_part(rows, values, chosen):
    adapters, tokens = chosen.shape
    terms = lax.dot_general(
        rows, values, (((1,), (1,)), ((), ())), preferred_element_type=jnp.float32
    )
    terms = terms.reshape(adapters, -1, tokens)
    return jnp.sum(jnp.where(chosen[:, None, :], terms, jnp.zeros((), jnp.float32)), axis=0)


def spread(chosen, low):
    adapters, tokens = chosen.shape
    wide = jnp.where(chosen[:, None, :], low[None], jnp.zeros((), low.dtype))
    return wide.reshape(adapters * low.shape[0], tokens)


def sum_over_tensor(part, size):
    if not power_of_two(size) or size > 4:
        return lax.psum(part, "tensor")
    terms = [part] + [lax.ppermute(part, "tensor", pairs(size, d)) for d in range(1, size)]
    while len(terms) > 1:
        terms = [terms[i] + terms[i + 1] for i in range(0, len(terms), 2)]
    return terms[0]


def reduce_to_owner(term_a, term_b, size):
    if size != 4:
        return tuple(
            lax.psum_scatter(t, "dp", scatter_dimension=0, tiled=True) for t in (term_a, term_b)
        )
    for distance in (1, 2):
        half = term_a.shape[0] // 2
        got_a = lax.ppermute(term_a[:half], "dp", pairs(size, distance))
        got_b = lax.ppermute(term_b[:half], "dp", pairs(size, distance))
        term_a = term_a[half:] + got_a
        term_b = term_b[half:] + got_b
    return term_a, term_b


def per_device(
    attention_output,
    projection_output_gradient,
    token_adapter_index,
    owner_slot_adapter,
    output_projection_weight,
    adapter_down_weight,
    adapter_up_weight,
):
    adapters, rank, attention_columns = adapter_down_weight.shape
    width_columns = adapter_up_weight.shape[2]
    tokens = attention_output.shape[0]
    tensor_size = lax.axis_size("tensor")
    dp_size = lax.axis_size("dp")
    input_rows = adapter_down_weight.reshape(adapters * rank, attention_columns)
    output_rows = adapter_up_weight.reshape(adapters * rank, width_columns)
    labels = jnp.arange(adapters, dtype=jnp.int32)
    chosen = labels[:, None] == token_adapter_index[None, :]
    row_dims = (((1,), (1,)), ((), ()))

    full_gradient = lax.all_gather(projection_output_gradient, "tensor", axis=1, tiled=True)

    out_part = low_rank_part(output_rows, projection_output_gradient, chosen)
    in_part = low_rank_part(input_rows, attention_output, chosen)
    low = sum_over_tensor(jnp.concatenate([in_part, out_part], axis=0), tensor_size)
    low_b = low.astype(jnp.bfloat16)
    in_b, out_b = low_b[:rank], low_b[rank:]

    if dp_size == 4:
        order = jnp.array([3, 1, 2, 0], jnp.int32) ^ lax.axis_index("dp")
        slots = owner_slot_adapter.reshape(dp_size, -1)[order].reshape(-1)
    else:
        slots = owner_slot_adapter
    owned = slots[:, None] == token_adapter_index[None, :]
    multiplier = ADAPTER_SCALE * OBJECTIVE_WEIGHT
    term_a = multiplier * jnp.dot(
        spread(owned, out_b), attention_output, preferred_element_type=jnp.float32
    )
    term_b = multiplier * jnp.dot(
        spread(owned, in_b), projection_output_gradient, preferred_element_type=jnp.float32
    )
    grad_a, grad_b = reduce_to_owner(term_a, term_b, dp_size)
    grad_a = grad_a.reshape(-1, rank, attention_columns)
    grad_b = grad_b.reshape(-1, rank, width_columns)

    wide = spread(chosen, out_b)
    contribution = lax.dot_general(
        wide, input_rows, (((0,), (0,)), ((), ())), preferred_element_type=jnp.float32
    )
    frozen = lax.dot_general(
        full_gradient, output_projection_weight, row_dims, preferred_element_type=jnp.float32
    )
    attention_gradient = (frozen + ADAPTER_SCALE * contribution).astype(jnp.bfloat16)
    return attention_gradient, grad_a, grad_b


def solution(mesh):
    placed = (
        P(("parts", "dp"), "tensor"),
        P(("parts", "dp"), "tensor"),
        P(("parts", "dp")),
        P(),
        P("tensor", None),
        P(None, None, "tensor"),
        P(None, None, "tensor"),
    )
    return jax.shard_map(
        per_device,
        mesh=mesh,
        in_specs=placed,
        out_specs=(
            P(("parts", "dp"), "tensor"),
            P(("parts", "dp"), None, "tensor"),
            P(("parts", "dp"), None, "tensor"),
        ),
        check_vma=False,
    )
```

```python
import functools

import jax
import jax.numpy as jnp
from jax import lax
from jax.experimental import pallas as pl
from jax.experimental.pallas import tpu as pltpu
from jax.sharding import PartitionSpec as P

ADAPTER_SCALE = 2.0
OBJECTIVE_WEIGHT = 0.05

TO_ENDS = [(1, 0), (2, 3)]
MIDDLES = [(1, 2), (2, 1)]
FLIP_X, FLIP_CORE = 2, 1
LAST = (((1,), (1,)), ((), ()))
FIRST = (((0,), (0,)), ((), ()))
PLAIN = (((1,), (0,)), ((), ()))


def pairs(size, distance):
    return [(i, i ^ distance) for i in range(size)]


def power_of_two(size):
    return size & (size - 1) == 0


def low_rank_part(rows, values, chosen):
    adapters, tokens = chosen.shape
    terms = lax.dot_general(
        rows, values, (((1,), (1,)), ((), ())), preferred_element_type=jnp.float32
    )
    terms = terms.reshape(adapters, -1, tokens)
    return jnp.sum(jnp.where(chosen[:, None, :], terms, jnp.zeros((), jnp.float32)), axis=0)


def spread(chosen, low):
    adapters, tokens = chosen.shape
    wide = jnp.where(chosen[:, None, :], low[None], jnp.zeros((), low.dtype))
    return wide.reshape(adapters * low.shape[0], tokens)


def sum_over_tensor(part, size):
    if not power_of_two(size) or size > 4:
        return lax.psum(part, "tensor")
    terms = [part] + [lax.ppermute(part, "tensor", pairs(size, d)) for d in range(1, size)]
    while len(terms) > 1:
        terms = [terms[i] + terms[i + 1] for i in range(0, len(terms), 2)]
    return terms[0]


def reduce_to_owner(term_a, term_b, size):
    if size != 4:
        return tuple(
            lax.psum_scatter(t, "dp", scatter_dimension=0, tiled=True) for t in (term_a, term_b)
        )
    for distance in (1, 2):
        half = term_a.shape[0] // 2
        got_a = lax.ppermute(term_a[:half], "dp", pairs(size, distance))
        got_b = lax.ppermute(term_b[:half], "dp", pairs(size, distance))
        term_a = term_a[half:] + got_a
        term_b = term_b[half:] + got_b
    return term_a, term_b


def general_device(
    attention_output,
    projection_output_gradient,
    token_adapter_index,
    owner_slot_adapter,
    output_projection_weight,
    adapter_down_weight,
    adapter_up_weight,
):
    adapters, rank, attention_columns = adapter_down_weight.shape
    width_columns = adapter_up_weight.shape[2]
    tokens = attention_output.shape[0]
    tensor_size = lax.axis_size("tensor")
    dp_size = lax.axis_size("dp")
    input_rows = adapter_down_weight.reshape(adapters * rank, attention_columns)
    output_rows = adapter_up_weight.reshape(adapters * rank, width_columns)
    labels = jnp.arange(adapters, dtype=jnp.int32)
    chosen = labels[:, None] == token_adapter_index[None, :]
    row_dims = (((1,), (1,)), ((), ()))

    full_gradient = lax.all_gather(projection_output_gradient, "tensor", axis=1, tiled=True)

    out_part = low_rank_part(output_rows, projection_output_gradient, chosen)
    in_part = low_rank_part(input_rows, attention_output, chosen)
    low = sum_over_tensor(jnp.concatenate([in_part, out_part], axis=0), tensor_size)
    low_b = low.astype(jnp.bfloat16)
    in_b, out_b = low_b[:rank], low_b[rank:]

    if dp_size == 4:
        order = jnp.array([3, 1, 2, 0], jnp.int32) ^ lax.axis_index("dp")
        slots = owner_slot_adapter.reshape(dp_size, -1)[order].reshape(-1)
    else:
        slots = owner_slot_adapter
    owned = slots[:, None] == token_adapter_index[None, :]
    multiplier = ADAPTER_SCALE * OBJECTIVE_WEIGHT
    term_a = multiplier * jnp.dot(
        spread(owned, out_b), attention_output, preferred_element_type=jnp.float32
    )
    term_b = multiplier * jnp.dot(
        spread(owned, in_b), projection_output_gradient, preferred_element_type=jnp.float32
    )
    grad_a, grad_b = reduce_to_owner(term_a, term_b, dp_size)
    grad_a = grad_a.reshape(-1, rank, attention_columns)
    grad_b = grad_b.reshape(-1, rank, width_columns)

    wide = spread(chosen, out_b)
    contribution = lax.dot_general(
        wide, input_rows, (((0,), (0,)), ((), ())), preferred_element_type=jnp.float32
    )
    frozen = lax.dot_general(
        full_gradient, output_projection_weight, row_dims, preferred_element_type=jnp.float32
    )
    attention_gradient = (frozen + ADAPTER_SCALE * contribution).astype(jnp.bfloat16)
    return attention_gradient, grad_a, grad_b


def dot(a, b, dims):
    return lax.dot_general(a, b, dims, preferred_element_type=jnp.float32)


def kernel_call(body, **kwargs):
    return pl.pallas_call(
        body,
        compiler_params=pltpu.CompilerParams(vmem_limit_bytes=56 << 20),
        cost_estimate=pl.CostEstimate(flops=1 << 20, bytes_accessed=1 << 16, transcendentals=0),
        **kwargs,
    )


def together(*arrays):
    return lax.optimization_barrier(arrays)


def whole(array):
    return pl.BlockSpec(array.shape, lambda i, *_: (0,) * array.ndim)


def low_rank_kernel(rank, _, index_ref, down_ref, values_ref, up_ref, gradient_ref, out_ref):
    rows, tokens = down_ref.shape[0], values_ref.shape[0]
    step = pl.program_id(0)

    @pl.when(step == 0)
    def _():
        out_ref[...] = jnp.zeros_like(out_ref)

    adapter = lax.broadcasted_iota(jnp.int32, (rows // rank, 1, tokens), 0) + step * (rows // rank)
    chosen = adapter == index_ref[...][None]
    for at, weight, values in ((0, down_ref, values_ref), (rank, up_ref, gradient_ref)):
        terms = dot(weight[...], values[...], LAST).reshape(rows // rank, rank, tokens)
        out_ref[at : at + rank] += jnp.sum(jnp.where(chosen, terms, 0.0), axis=0)


def low_rank(after, index, down, values, up, gradient, rank):
    tokens = values.shape[0]
    rows = down.shape[0]
    block = rows // 4
    return kernel_call(
        functools.partial(low_rank_kernel, rank),
        grid=(4,),
        in_specs=[
            pl.BlockSpec(memory_space=pl.ANY),
            whole(index),
            pl.BlockSpec((block, down.shape[1]), lambda i: (i, 0)),
            whole(values),
            pl.BlockSpec((block, up.shape[1]), lambda i: (i, 0)),
            whole(gradient),
        ],
        out_specs=pl.BlockSpec((2 * rank, tokens), lambda i: (0, 0)),
        out_shape=jax.ShapeDtypeStruct((2 * rank, tokens), jnp.float32),
    )(after, index, down, values, up, gradient)


def spread_rows(labels, index, low):
    wide = jnp.concatenate([low] * (labels.shape[0] // low.shape[0]), axis=0)
    return jnp.where(labels == index, wide, 0.0).astype(jnp.bfloat16)


def adapter_gradient_kernel(
    slots_ref, index_ref, low0, low1, low2, low3, values_ref, gradient_ref, send_ref, keep_ref, low_ref
):
    step = pl.program_id(0)

    @pl.when(step == 0)
    def _():
        low_ref[...] = (low0[...] + low1[...]) + (low2[...] + low3[...])

    rank = low_ref.shape[0] // 2
    low = low_ref[...].astype(jnp.bfloat16).astype(jnp.float32)
    multiplier = ADAPTER_SCALE * OBJECTIVE_WEIGHT
    a = multiplier * dot(
        spread_rows(slots_ref[...], index_ref[...], low[rank:]), values_ref[...], PLAIN
    )
    b = multiplier * dot(
        spread_rows(slots_ref[...], index_ref[...], low[:rank]), gradient_ref[...], PLAIN
    )
    split = a.shape[1]

    @pl.when(step < 2)
    def _():
        send_ref[:, :split] = a
        send_ref[:, split:] = b

    @pl.when(step >= 2)
    def _():
        keep_ref[:, :split] = a
        keep_ref[:, split:] = b


def adapter_gradients(slots, index, low_terms, values, gradient):
    rows = slots.shape[0]
    block = rows // 4
    width = values.shape[1] + gradient.shape[1]
    half = jax.ShapeDtypeStruct((rows // 2, width), jnp.float32)
    return kernel_call(
        adapter_gradient_kernel,
        grid=(4,),
        in_specs=[
            pl.BlockSpec((block, 1), lambda i: (i, 0)),
            whole(index),
            *(whole(term) for term in low_terms),
            whole(values),
            whole(gradient),
        ],
        out_specs=[
            pl.BlockSpec((block, width), lambda i: (jnp.minimum(i, 1), 0)),
            pl.BlockSpec((block, width), lambda i: (jnp.maximum(i - 2, 0), 0)),
            whole(low_terms[0]),
        ],
        out_shape=[half, half, jax.ShapeDtypeStruct(low_terms[0].shape, jnp.float32)],
    )(slots, index, *low_terms, values, gradient)


def halves_kernel(keep_ref, got_ref, send_ref, out_ref):
    total = keep_ref[...] + got_ref[...]

    @pl.when(pl.program_id(0) < 2)
    def _():
        send_ref[...] = total.astype(send_ref.dtype)

    @pl.when(pl.program_id(0) >= 2)
    def _():
        out_ref[...] = total


def add_in_halves(keep, got):
    rows, width = keep.shape
    block = rows // 4
    both = pl.BlockSpec((block, width), lambda i: (i, 0))
    return kernel_call(
        halves_kernel,
        grid=(4,),
        in_specs=[both, both],
        out_specs=[
            pl.BlockSpec((block, width), lambda i: (jnp.minimum(i, 1), 0)),
            pl.BlockSpec((block, width), lambda i: (jnp.maximum(i - 2, 0), 0)),
        ],
        out_shape=[
            jax.ShapeDtypeStruct((rows // 2, width), jnp.bfloat16),
            jax.ShapeDtypeStruct((rows // 2, width), jnp.float32),
        ],
    )(keep, got)


def owned_kernel(keep_ref, got_ref, a_ref, b_ref):
    split = a_ref.shape[1]
    a_ref[...] = keep_ref[:, :split] + got_ref[:, :split].astype(jnp.float32)
    b_ref[...] = keep_ref[:, split:] + got_ref[:, split:].astype(jnp.float32)


def owned_sums(keep, got, split):
    rows, width = keep.shape
    block = rows // 4
    widths = (split, width - split)
    return kernel_call(
        owned_kernel,
        grid=(4,),
        in_specs=[pl.BlockSpec((block, width), lambda i: (i, 0))] * 2,
        out_specs=[pl.BlockSpec((block, w), lambda i: (i, 0)) for w in widths],
        out_shape=[jax.ShapeDtypeStruct((rows, w), jnp.float32) for w in widths],
    )(keep, got)


def rows_kernel(distances, with_adapters, here_ref, _, *refs):
    start_count = 3 if with_adapters else 1
    start_refs, refs = refs[:start_count], refs[start_count:]
    arrays, (weight_ref, out_ref, *scratch) = refs[: len(distances)], refs[len(distances) :]
    if with_adapters:
        index_ref, low_ref, rows_ref = start_refs
        (wide_ref,) = scratch

        @pl.when(pl.program_id(0) == 0)
        def _():
            rank = low_ref.shape[0] // 2
            labels = lax.broadcasted_iota(jnp.int32, wide_ref.shape[::-1], 0) // rank
            low = low_ref[rank:].astype(jnp.bfloat16).astype(jnp.float32)
            wide_ref[...] = spread_rows(labels, index_ref[...], low).T

        total = ADAPTER_SCALE * dot(wide_ref[...], rows_ref[...], PLAIN)
    else:
        total = start_refs[0][...]
    columns = arrays[0].shape[1]
    blocks = {}
    for distance, ref in zip(distances, arrays):
        blocks[distance] = blocks[distance] + ref[...] if distance in blocks else ref[...]
    for distance, block in blocks.items():
        if weight_ref.shape[1] == columns:
            total += dot(block, weight_ref[...], LAST)
        else:
            at = pl.multiple_of((here_ref[0] ^ distance) * columns, 128)
            total += dot(block, weight_ref[:, pl.ds(at, columns)], LAST)
    out_ref[...] = total.astype(out_ref.dtype)


def add_products(here, before, start, blocks, weight, first, tokens):
    step = blocks[0][1].shape[0]
    features, width = weight.shape
    block = 1024 if len(blocks) == 2 else 512
    here_at = first // step
    if before is None:
        out, at = jax.ShapeDtypeStruct((step, features), jnp.float32), 0
    else:
        out, at = jax.ShapeDtypeStruct((tokens, features), jnp.bfloat16), here_at
    distances, arrays = zip(*blocks)
    if len(set(distances)) == 1:
        weight_block = pl.BlockSpec(
            (block, arrays[0].shape[1]), lambda i, here: (i, here[0] ^ distances[0])
        )
    else:
        weight_block = pl.BlockSpec((block, width), lambda i, _: (i, 0))
    with_adapters = isinstance(start, tuple)
    if with_adapters:
        index, low, rows = start
        start_blocks = [
            pl.BlockSpec((1, step), lambda i, _: (0, here_at)),
            pl.BlockSpec((low.shape[0], step), lambda i, _: (0, here_at)),
            pl.BlockSpec((rows.shape[0], block), lambda i, _: (0, i)),
        ]
        scratch = [pltpu.VMEM((step, rows.shape[0]), jnp.bfloat16)]
    else:
        start = (start,)
        start_blocks = [pl.BlockSpec((step, block), lambda i, _: (0, i))]
        scratch = []
    return kernel_call(
        functools.partial(rows_kernel, distances, with_adapters),
        grid_spec=pltpu.PrefetchScalarGridSpec(
            num_scalar_prefetch=1,
            grid=(features // block,),
            in_specs=[
                pl.BlockSpec(memory_space=pl.ANY),
                *start_blocks,
                *(whole(b) for b in arrays),
                weight_block,
            ],
            out_specs=pl.BlockSpec((step, block), lambda i, _: (at, i)),
            scratch_shapes=scratch,
        ),
        out_shape=out,
        input_output_aliases={} if before is None or before is here else {1: 0},
    )(here, here if before is None else before, *start, *arrays, weight)


def line_device(
    attention_output,
    projection_output_gradient,
    token_adapter_index,
    owner_slot_adapter,
    output_projection_weight,
    adapter_down_weight,
    adapter_up_weight,
):
    adapters, rank, attention_columns = adapter_down_weight.shape
    columns = adapter_up_weight.shape[2]
    tokens = attention_output.shape[0]
    here = lax.axis_index("tensor")[None]
    down = adapter_down_weight.reshape(adapters * rank, attention_columns)
    up = adapter_up_weight.reshape(adapters * rank, columns)
    index = token_adapter_index[None, :]

    step = tokens // 2
    order = jnp.array([3, 1, 2, 0], jnp.int32) ^ lax.axis_index("dp")
    slots = jnp.repeat(owner_slot_adapter.reshape(4, -1)[order].reshape(-1), rank)[:, None]
    weight = output_projection_weight

    def swap(block):
        return lax.ppermute(block, "tensor", pairs(4, 1))

    def cross(block):
        return lax.ppermute(block, "tensor", MIDDLES)

    def to_end(block):
        return lax.ppermute(block, "tensor", TO_ENDS)

    own = [projection_output_gradient[c * step : (c + 1) * step] for c in range(2)]
    near, across, far, end_across, end_far = ({} for _ in range(5))

    near[0], across[0], near[1] = swap(own[0]), cross(own[0]), swap(own[1])
    low_part = low_rank(index, index, down, attention_output, up, projection_output_gradient, rank)
    low_part, near[0], across[0] = together(low_part, near[0], across[0])
    low_terms = [low_part] + [lax.ppermute(low_part, "tensor", pairs(4, d)) for d in (1, 2, 3)]
    far[0] = cross(near[0])
    near[1], far[0], across[0], own[1], *low_terms = together(
        near[1], far[0], across[0], own[1], *low_terms
    )
    across[1], end_across[0] = cross(own[1]), to_end(across[0])
    end_far[0], far[1] = to_end(far[0]), cross(near[1])
    send, keep, low = adapter_gradients(
        slots, index, low_terms, attention_output, projection_output_gradient
    )
    send, keep, end_across[0], across[1] = together(send, keep, end_across[0], across[1])
    got = lax.ppermute(send, "dp", pairs(4, FLIP_CORE))
    end_across[1] = to_end(across[1])
    to_x, keep = add_in_halves(keep, got)
    to_x, keep, end_far[0], far[1], index = together(to_x, keep, end_far[0], far[1], index)
    got = lax.ppermute(to_x, "dp", pairs(4, FLIP_X))
    end_far[1] = to_end(far[1])
    result = add_products(
        here,
        here,
        (index, low, down),
        ((0, own[0]), (1, near[0]), (2, far[0]), (2, end_across[0]), (3, across[0]), (3, end_far[0])),
        weight,
        0,
        tokens,
    )
    result, end_across[1], index, got = together(result, end_across[1], index, got)
    grad_a, grad_b = owned_sums(keep, got, attention_columns)
    base = add_products(
        here,
        None,
        (index, low, down),
        ((0, own[1]), (1, near[1]), (2, far[1]), (2, end_across[1])),
        weight,
        step,
        tokens,
    )
    grad_a, grad_b, base, end_far[1], result = together(grad_a, grad_b, base, end_far[1], result)
    result = add_products(
        here, result, base, ((3, across[1]), (3, end_far[1])), weight, step, tokens
    )
    grad_a = grad_a.reshape(-1, rank, attention_columns)
    grad_b = grad_b.reshape(-1, rank, columns)
    return result, grad_a, grad_b


def per_device(*arrays):
    sizes = tuple(lax.axis_size(a) for a in ("parts", "tensor", "dp"))
    tokens, attention_columns = arrays[0].shape
    columns = arrays[1].shape[1]
    fits = tokens % 1024 == 0 and attention_columns % 2048 == 0 and columns % 128 == 0
    if sizes == (2, 4, 4) and fits:
        return line_device(*arrays)
    return general_device(*arrays)


def solution(mesh):
    placed = (
        P(("parts", "dp"), "tensor"),
        P(("parts", "dp"), "tensor"),
        P(("parts", "dp")),
        P(),
        P("tensor", None),
        P(None, None, "tensor"),
        P(None, None, "tensor"),
    )
    return jax.shard_map(
        per_device,
        mesh=mesh,
        in_specs=placed,
        out_specs=(
            P(("parts", "dp"), "tensor"),
            P(("parts", "dp"), None, "tensor"),
            P(("parts", "dp"), None, "tensor"),
        ),
        check_vma=False,
    )
```

```python
import functools

import jax
import jax.numpy as jnp
from jax import lax
from jax.experimental import pallas as pl
from jax.experimental.pallas import tpu as pltpu
from jax.sharding import PartitionSpec as P

ADAPTER_SCALE = 2.0
OBJECTIVE_WEIGHT = 0.05
LAST_ROWS = 256
FIRST_EIGHTHS = 3

TO_ENDS = [(1, 0), (2, 3)]
MIDDLES = [(1, 2), (2, 1)]
FLIP_X, FLIP_CORE = 2, 1
LAST = (((1,), (1,)), ((), ()))
FIRST = (((0,), (0,)), ((), ()))
PLAIN = (((1,), (0,)), ((), ()))


def pairs(size, distance):
    return [(i, i ^ distance) for i in range(size)]


def power_of_two(size):
    return size & (size - 1) == 0


def low_rank_part(rows, values, chosen):
    adapters, tokens = chosen.shape
    terms = lax.dot_general(
        rows, values, (((1,), (1,)), ((), ())), preferred_element_type=jnp.float32
    )
    terms = terms.reshape(adapters, -1, tokens)
    return jnp.sum(jnp.where(chosen[:, None, :], terms, jnp.zeros((), jnp.float32)), axis=0)


def spread(chosen, low):
    adapters, tokens = chosen.shape
    wide = jnp.where(chosen[:, None, :], low[None], jnp.zeros((), low.dtype))
    return wide.reshape(adapters * low.shape[0], tokens)


def sum_over_tensor(part, size):
    if not power_of_two(size) or size > 4:
        return lax.psum(part, "tensor")
    terms = [part] + [lax.ppermute(part, "tensor", pairs(size, d)) for d in range(1, size)]
    while len(terms) > 1:
        terms = [terms[i] + terms[i + 1] for i in range(0, len(terms), 2)]
    return terms[0]


def reduce_to_owner(term_a, term_b, size):
    if size != 4:
        return tuple(
            lax.psum_scatter(t, "dp", scatter_dimension=0, tiled=True) for t in (term_a, term_b)
        )
    for distance in (1, 2):
        half = term_a.shape[0] // 2
        got_a = lax.ppermute(term_a[:half], "dp", pairs(size, distance))
        got_b = lax.ppermute(term_b[:half], "dp", pairs(size, distance))
        term_a = term_a[half:] + got_a
        term_b = term_b[half:] + got_b
    return term_a, term_b


def general_device(
    attention_output,
    projection_output_gradient,
    token_adapter_index,
    owner_slot_adapter,
    output_projection_weight,
    adapter_down_weight,
    adapter_up_weight,
):
    adapters, rank, attention_columns = adapter_down_weight.shape
    width_columns = adapter_up_weight.shape[2]
    tokens = attention_output.shape[0]
    tensor_size = lax.axis_size("tensor")
    dp_size = lax.axis_size("dp")
    input_rows = adapter_down_weight.reshape(adapters * rank, attention_columns)
    output_rows = adapter_up_weight.reshape(adapters * rank, width_columns)
    labels = jnp.arange(adapters, dtype=jnp.int32)
    chosen = labels[:, None] == token_adapter_index[None, :]
    row_dims = (((1,), (1,)), ((), ()))

    full_gradient = lax.all_gather(projection_output_gradient, "tensor", axis=1, tiled=True)

    out_part = low_rank_part(output_rows, projection_output_gradient, chosen)
    in_part = low_rank_part(input_rows, attention_output, chosen)
    low = sum_over_tensor(jnp.concatenate([in_part, out_part], axis=0), tensor_size)
    low_b = low.astype(jnp.bfloat16)
    in_b, out_b = low_b[:rank], low_b[rank:]

    if dp_size == 4:
        order = jnp.array([3, 1, 2, 0], jnp.int32) ^ lax.axis_index("dp")
        slots = owner_slot_adapter.reshape(dp_size, -1)[order].reshape(-1)
    else:
        slots = owner_slot_adapter
    owned = slots[:, None] == token_adapter_index[None, :]
    multiplier = ADAPTER_SCALE * OBJECTIVE_WEIGHT
    term_a = multiplier * jnp.dot(
        spread(owned, out_b), attention_output, preferred_element_type=jnp.float32
    )
    term_b = multiplier * jnp.dot(
        spread(owned, in_b), projection_output_gradient, preferred_element_type=jnp.float32
    )
    grad_a, grad_b = reduce_to_owner(term_a, term_b, dp_size)
    grad_a = grad_a.reshape(-1, rank, attention_columns)
    grad_b = grad_b.reshape(-1, rank, width_columns)

    wide = spread(chosen, out_b)
    contribution = lax.dot_general(
        wide, input_rows, (((0,), (0,)), ((), ())), preferred_element_type=jnp.float32
    )
    frozen = lax.dot_general(
        full_gradient, output_projection_weight, row_dims, preferred_element_type=jnp.float32
    )
    attention_gradient = (frozen + ADAPTER_SCALE * contribution).astype(jnp.bfloat16)
    return attention_gradient, grad_a, grad_b


def dot(a, b, dims):
    return lax.dot_general(a, b, dims, preferred_element_type=jnp.float32)


def kernel_call(body, **kwargs):
    return pl.pallas_call(
        body,
        compiler_params=pltpu.CompilerParams(vmem_limit_bytes=62 << 20),
        cost_estimate=pl.CostEstimate(flops=1 << 20, bytes_accessed=1 << 16, transcendentals=0),
        **kwargs,
    )


def together(*arrays):
    return lax.optimization_barrier(arrays)


def whole(array):
    return pl.BlockSpec(array.shape, lambda i, *_: (0,) * array.ndim)


def low_rank_kernel(rank, _, index_ref, down_ref, values_ref, up_ref, gradient_ref, out_ref):
    rows, tokens = down_ref.shape[0], values_ref.shape[0]
    step = pl.program_id(0)

    @pl.when(step == 0)
    def _():
        out_ref[...] = jnp.zeros_like(out_ref)

    adapter = lax.broadcasted_iota(jnp.int32, (rows // rank, 1, tokens), 0) + step * (rows // rank)
    chosen = adapter == index_ref[...][None]
    for at, weight, values in ((0, down_ref, values_ref), (rank, up_ref, gradient_ref)):
        terms = dot(weight[...], values[...], LAST).reshape(rows // rank, rank, tokens)
        out_ref[at : at + rank] += jnp.sum(jnp.where(chosen, terms, 0.0), axis=0)


def low_rank(after, index, down, values, up, gradient, rank):
    tokens = values.shape[0]
    rows = down.shape[0]
    block = rows // 4
    return kernel_call(
        functools.partial(low_rank_kernel, rank),
        grid=(4,),
        in_specs=[
            pl.BlockSpec(memory_space=pl.ANY),
            whole(index),
            pl.BlockSpec((block, down.shape[1]), lambda i: (i, 0)),
            whole(values),
            pl.BlockSpec((block, up.shape[1]), lambda i: (i, 0)),
            whole(gradient),
        ],
        out_specs=pl.BlockSpec((2 * rank, tokens), lambda i: (0, 0)),
        out_shape=jax.ShapeDtypeStruct((2 * rank, tokens), jnp.float32),
    )(after, index, down, values, up, gradient)


def spread_rows(labels, index, low):
    wide = jnp.concatenate([low] * (labels.shape[0] // low.shape[0]), axis=0)
    return jnp.where(labels == index, wide, 0.0).astype(jnp.bfloat16)


def adapter_gradient_kernel(
    slots_ref, index_ref, low0, low1, low2, low3, values_ref, gradient_ref, send_ref, keep_ref, low_ref
):
    step = pl.program_id(0)

    @pl.when(step == 0)
    def _():
        low_ref[...] = (low0[...] + low1[...]) + (low2[...] + low3[...])

    rank = low_ref.shape[0] // 2
    low = low_ref[...].astype(jnp.bfloat16).astype(jnp.float32)
    multiplier = ADAPTER_SCALE * OBJECTIVE_WEIGHT
    a = multiplier * dot(
        spread_rows(slots_ref[...], index_ref[...], low[rank:]), values_ref[...], PLAIN
    )
    b = multiplier * dot(
        spread_rows(slots_ref[...], index_ref[...], low[:rank]), gradient_ref[...], PLAIN
    )
    split = a.shape[1]

    @pl.when(step < 2)
    def _():
        send_ref[:, :split] = a
        send_ref[:, split:] = b

    @pl.when(step >= 2)
    def _():
        keep_ref[:, :split] = a
        keep_ref[:, split:] = b


def adapter_gradients(slots, index, low_terms, values, gradient):
    rows = slots.shape[0]
    block = rows // 4
    width = values.shape[1] + gradient.shape[1]
    half = jax.ShapeDtypeStruct((rows // 2, width), jnp.float32)
    return kernel_call(
        adapter_gradient_kernel,
        grid=(4,),
        in_specs=[
            pl.BlockSpec((block, 1), lambda i: (i, 0)),
            whole(index),
            *(whole(term) for term in low_terms),
            whole(values),
            whole(gradient),
        ],
        out_specs=[
            pl.BlockSpec((block, width), lambda i: (jnp.minimum(i, 1), 0)),
            pl.BlockSpec((block, width), lambda i: (jnp.maximum(i - 2, 0), 0)),
            whole(low_terms[0]),
        ],
        out_shape=[half, half, jax.ShapeDtypeStruct(low_terms[0].shape, jnp.float32)],
    )(slots, index, *low_terms, values, gradient)


def halves_kernel(keep_ref, got_ref, send_ref, out_ref):
    total = keep_ref[...] + got_ref[...]

    @pl.when(pl.program_id(0) < 2)
    def _():
        send_ref[...] = total.astype(send_ref.dtype)

    @pl.when(pl.program_id(0) >= 2)
    def _():
        out_ref[...] = total


def add_in_halves(keep, got):
    rows, width = keep.shape
    block = rows // 4
    both = pl.BlockSpec((block, width), lambda i: (i, 0))
    return kernel_call(
        halves_kernel,
        grid=(4,),
        in_specs=[both, both],
        out_specs=[
            pl.BlockSpec((block, width), lambda i: (jnp.minimum(i, 1), 0)),
            pl.BlockSpec((block, width), lambda i: (jnp.maximum(i - 2, 0), 0)),
        ],
        out_shape=[
            jax.ShapeDtypeStruct((rows // 2, width), jnp.bfloat16),
            jax.ShapeDtypeStruct((rows // 2, width), jnp.float32),
        ],
    )(keep, got)


def owned_kernel(keep_ref, got_ref, a_ref, b_ref):
    split = a_ref.shape[1]
    a_ref[...] = keep_ref[:, :split] + got_ref[:, :split].astype(jnp.float32)
    b_ref[...] = keep_ref[:, split:] + got_ref[:, split:].astype(jnp.float32)


def owned_sums(keep, got, split):
    rows, width = keep.shape
    block = rows // 4
    widths = (split, width - split)
    return kernel_call(
        owned_kernel,
        grid=(4,),
        in_specs=[pl.BlockSpec((block, width), lambda i: (i, 0))] * 2,
        out_specs=[pl.BlockSpec((block, w), lambda i: (i, 0)) for w in widths],
        out_shape=[jax.ShapeDtypeStruct((rows, w), jnp.float32) for w in widths],
    )(keep, got)


def rows_kernel(distances, first, here_ref, _, *refs):
    with_adapters = first is not None
    start_count = 3 if with_adapters else 1
    start_refs, refs = refs[:start_count], refs[start_count:]
    arrays, (weight_ref, out_ref, *scratch) = refs[: len(distances)], refs[len(distances) :]
    if with_adapters:
        index_ref, low_ref, rows_ref = start_refs
        (wide_ref,) = scratch

        @pl.when(pl.program_id(0) == 0)
        def _():
            rank = low_ref.shape[0] // 2
            labels = lax.broadcasted_iota(jnp.int32, wide_ref.shape[::-1], 0) // rank
            here_tokens = pl.ds(first, wide_ref.shape[0])
            low = low_ref[rank:, here_tokens].astype(jnp.bfloat16).astype(jnp.float32)
            wide_ref[...] = spread_rows(labels, index_ref[:, here_tokens], low).T

        total = ADAPTER_SCALE * dot(wide_ref[...], rows_ref[...], PLAIN)
    else:
        total = start_refs[0][...]
    columns = arrays[0].shape[1]
    blocks = {}
    for distance, ref in zip(distances, arrays):
        blocks[distance] = blocks[distance] + ref[...] if distance in blocks else ref[...]
    for distance, block in blocks.items():
        if weight_ref.shape[1] == columns:
            total += dot(block, weight_ref[...], LAST)
        else:
            at = pl.multiple_of((here_ref[0] ^ distance) * columns, 128)
            total += dot(block, weight_ref[:, pl.ds(at, columns)], LAST)
    out_ref[...] = total.astype(out_ref.dtype)


def add_products(here, before, start, blocks, weight, first, tokens, skip=0):
    step = blocks[-1][1].shape[0]
    features, width = weight.shape
    block = 1024 if len(blocks) == 2 else 512
    if before is None:
        out = jax.ShapeDtypeStruct((step, features), jnp.float32)
        out_block = pl.BlockSpec((step, block), lambda i, _: (0, i))
    elif first == 0:
        out = jax.ShapeDtypeStruct((tokens, features), jnp.bfloat16)
        out_block = pl.BlockSpec((step, block), lambda i, _: (0, i))
    else:
        out = jax.ShapeDtypeStruct((tokens, features), jnp.bfloat16)
        out_block = pl.BlockSpec(
            (pl.Element(step), pl.Element(block)), lambda i, _: (first, i * block)
        )
    distances, arrays = zip(*blocks)
    if len(set(distances)) == 1:
        weight_block = pl.BlockSpec(
            (block, arrays[0].shape[1]), lambda i, here: (i, here[0] ^ distances[0])
        )
    else:
        weight_block = pl.BlockSpec((block, width), lambda i, _: (i, 0))
    with_adapters = isinstance(start, tuple)
    if with_adapters:
        index, low, rows = start
        start_blocks = [
            whole(index),
            whole(low),
            pl.BlockSpec((rows.shape[0], block), lambda i, _: (0, i)),
        ]
        scratch = [pltpu.VMEM((step, rows.shape[0]), jnp.bfloat16)]
    else:
        start = (start,)
        start_blocks = [
            pl.BlockSpec((pl.Element(step), pl.Element(block)), lambda i, _: (skip, i * block))
        ]
        scratch = []
    return kernel_call(
        functools.partial(rows_kernel, distances, first if with_adapters else None),
        grid_spec=pltpu.PrefetchScalarGridSpec(
            num_scalar_prefetch=1,
            grid=(features // block,),
            in_specs=[
                pl.BlockSpec(memory_space=pl.ANY),
                *start_blocks,
                *(
                    pl.BlockSpec(
                        (pl.Element(step), pl.Element(b.shape[1])),
                        lambda i, _, b=b: (skip if b.shape[0] > step else 0, 0),
                    )
                    for b in arrays
                ),
                weight_block,
            ],
            out_specs=out_block,
            scratch_shapes=scratch,
        ),
        out_shape=out,
        input_output_aliases={} if before is None or before is here else {1: 0},
    )(here, here if before is None else before, *start, *arrays, weight)


def line_device(
    attention_output,
    projection_output_gradient,
    token_adapter_index,
    owner_slot_adapter,
    output_projection_weight,
    adapter_down_weight,
    adapter_up_weight,
):
    adapters, rank, attention_columns = adapter_down_weight.shape
    columns = adapter_up_weight.shape[2]
    tokens = attention_output.shape[0]
    here = lax.axis_index("tensor")[None]
    down = adapter_down_weight.reshape(adapters * rank, attention_columns)
    up = adapter_up_weight.reshape(adapters * rank, columns)
    index = token_adapter_index[None, :]

    cut = tokens * FIRST_EIGHTHS // 8
    order = jnp.array([3, 1, 2, 0], jnp.int32) ^ lax.axis_index("dp")
    slots = jnp.repeat(owner_slot_adapter.reshape(4, -1)[order].reshape(-1), rank)[:, None]
    weight = output_projection_weight

    def swap(block):
        return lax.ppermute(block, "tensor", pairs(4, 1))

    def cross(block):
        return lax.ppermute(block, "tensor", MIDDLES)

    def to_end(block):
        return lax.ppermute(block, "tensor", TO_ENDS)

    own = [projection_output_gradient[:cut], projection_output_gradient[cut:]]
    near, across, far, end_across, end_far = ({} for _ in range(5))

    near[0], across[0] = swap(own[0]), cross(own[0])
    low_part = low_rank(index, index, down, attention_output, up, projection_output_gradient, rank)
    low_terms = [low_part] + [lax.ppermute(low_part, "tensor", pairs(4, d)) for d in (1, 2, 3)]
    near[0], across[0], own[1], *low_terms = together(near[0], across[0], own[1], *low_terms)
    near[1], far[0] = swap(own[1]), cross(near[0])
    send, keep, low = adapter_gradients(
        slots, index, low_terms, attention_output, projection_output_gradient
    )
    send, keep, near[1], far[0], across[0], own[1], index = together(
        send, keep, near[1], far[0], across[0], own[1], index
    )
    end_across[0], across[1] = to_end(across[0]), cross(own[1])
    got = lax.ppermute(send, "dp", pairs(4, FLIP_CORE))
    end_far[0], far[1] = to_end(far[0]), cross(near[1])
    to_x, keep = add_in_halves(keep, got)
    to_x, keep, end_across[0], across[1], index = together(
        to_x, keep, end_across[0], across[1], index
    )
    got = lax.ppermute(to_x, "dp", pairs(4, FLIP_X))
    end_across[1] = to_end(across[1])
    base0 = add_products(
        here,
        None,
        (index, low, down),
        ((0, own[0]), (1, near[0]), (2, far[0]), (2, end_across[0])),
        weight,
        0,
        tokens,
    )
    base0, end_far[0] = together(base0, end_far[0])
    result = add_products(
        here, here, base0, ((3, across[0]), (3, end_far[0])), weight, 0, tokens
    )
    result, far[1], index = together(result, far[1], index)
    tail = far[1].shape[0] - LAST_ROWS
    end_far[1], end_far[2] = to_end(far[1][:tail]), to_end(far[1][tail:])
    grad_a, grad_b = owned_sums(keep, got, attention_columns)
    grad_a, grad_b, end_across[1], index = together(grad_a, grad_b, end_across[1], index)
    base = add_products(
        here,
        None,
        (index, low, down),
        ((0, own[1]), (1, near[1]), (2, far[1]), (2, end_across[1])),
        weight,
        cut,
        tokens,
    )
    base, end_far[1], result = together(base, end_far[1], result)
    result = add_products(
        here, result, base, ((3, across[1]), (3, end_far[1])), weight, cut, tokens
    )
    result, end_far[2] = together(result, end_far[2])
    result = add_products(
        here, result, base, ((3, across[1]), (3, end_far[2])), weight, cut + tail, tokens, tail
    )
    grad_a = grad_a.reshape(-1, rank, attention_columns)
    grad_b = grad_b.reshape(-1, rank, columns)
    return result, grad_a, grad_b


def per_device(*arrays):
    sizes = tuple(lax.axis_size(a) for a in ("parts", "tensor", "dp"))
    tokens, attention_columns = arrays[0].shape
    columns = arrays[1].shape[1]
    fits = tokens % 1024 == 0 and attention_columns % 2048 == 0 and columns % 128 == 0
    if sizes == (2, 4, 4) and fits:
        return line_device(*arrays)
    return general_device(*arrays)


def solution(mesh):
    placed = (
        P(("parts", "dp"), "tensor"),
        P(("parts", "dp"), "tensor"),
        P(("parts", "dp")),
        P(),
        P("tensor", None),
        P(None, None, "tensor"),
        P(None, None, "tensor"),
    )
    return jax.shard_map(
        per_device,
        mesh=mesh,
        in_specs=placed,
        out_specs=(
            P(("parts", "dp"), "tensor"),
            P(("parts", "dp"), None, "tensor"),
            P(("parts", "dp"), None, "tensor"),
        ),
        check_vma=False,
    )
```

```python
import functools

import jax
import jax.numpy as jnp
from jax import lax
from jax.experimental import pallas as pl
from jax.experimental.pallas import tpu as pltpu
from jax.sharding import PartitionSpec as P

ADAPTER_SCALE = 2.0
OBJECTIVE_WEIGHT = 0.05
LAST_ROWS = 256
PIECE = 128
FIRST_EIGHTHS = 3

TO_ENDS = [(1, 0), (2, 3)]
MIDDLES = [(1, 2), (2, 1)]
FLIP_X, FLIP_CORE = 2, 1
LAST = (((1,), (1,)), ((), ()))
FIRST = (((0,), (0,)), ((), ()))
PLAIN = (((1,), (0,)), ((), ()))


def pairs(size, distance):
    return [(i, i ^ distance) for i in range(size)]


def power_of_two(size):
    return size & (size - 1) == 0


def low_rank_part(rows, values, chosen):
    adapters, tokens = chosen.shape
    terms = lax.dot_general(
        rows, values, (((1,), (1,)), ((), ())), preferred_element_type=jnp.float32
    )
    terms = terms.reshape(adapters, -1, tokens)
    return jnp.sum(jnp.where(chosen[:, None, :], terms, jnp.zeros((), jnp.float32)), axis=0)


def spread(chosen, low):
    adapters, tokens = chosen.shape
    wide = jnp.where(chosen[:, None, :], low[None], jnp.zeros((), low.dtype))
    return wide.reshape(adapters * low.shape[0], tokens)


def sum_over_tensor(part, size):
    if not power_of_two(size) or size > 4:
        return lax.psum(part, "tensor")
    terms = [part] + [lax.ppermute(part, "tensor", pairs(size, d)) for d in range(1, size)]
    while len(terms) > 1:
        terms = [terms[i] + terms[i + 1] for i in range(0, len(terms), 2)]
    return terms[0]


def reduce_to_owner(term_a, term_b, size):
    if size != 4:
        return tuple(
            lax.psum_scatter(t, "dp", scatter_dimension=0, tiled=True) for t in (term_a, term_b)
        )
    for distance in (1, 2):
        half = term_a.shape[0] // 2
        got_a = lax.ppermute(term_a[:half], "dp", pairs(size, distance))
        got_b = lax.ppermute(term_b[:half], "dp", pairs(size, distance))
        term_a = term_a[half:] + got_a
        term_b = term_b[half:] + got_b
    return term_a, term_b


def general_device(
    attention_output,
    projection_output_gradient,
    token_adapter_index,
    owner_slot_adapter,
    output_projection_weight,
    adapter_down_weight,
    adapter_up_weight,
):
    adapters, rank, attention_columns = adapter_down_weight.shape
    width_columns = adapter_up_weight.shape[2]
    tokens = attention_output.shape[0]
    tensor_size = lax.axis_size("tensor")
    dp_size = lax.axis_size("dp")
    input_rows = adapter_down_weight.reshape(adapters * rank, attention_columns)
    output_rows = adapter_up_weight.reshape(adapters * rank, width_columns)
    labels = jnp.arange(adapters, dtype=jnp.int32)
    chosen = labels[:, None] == token_adapter_index[None, :]
    row_dims = (((1,), (1,)), ((), ()))

    full_gradient = lax.all_gather(projection_output_gradient, "tensor", axis=1, tiled=True)

    out_part = low_rank_part(output_rows, projection_output_gradient, chosen)
    in_part = low_rank_part(input_rows, attention_output, chosen)
    low = sum_over_tensor(jnp.concatenate([in_part, out_part], axis=0), tensor_size)
    low_b = low.astype(jnp.bfloat16)
    in_b, out_b = low_b[:rank], low_b[rank:]

    if dp_size == 4:
        order = jnp.array([3, 1, 2, 0], jnp.int32) ^ lax.axis_index("dp")
        slots = owner_slot_adapter.reshape(dp_size, -1)[order].reshape(-1)
    else:
        slots = owner_slot_adapter
    owned = slots[:, None] == token_adapter_index[None, :]
    multiplier = ADAPTER_SCALE * OBJECTIVE_WEIGHT
    term_a = multiplier * jnp.dot(
        spread(owned, out_b), attention_output, preferred_element_type=jnp.float32
    )
    term_b = multiplier * jnp.dot(
        spread(owned, in_b), projection_output_gradient, preferred_element_type=jnp.float32
    )
    grad_a, grad_b = reduce_to_owner(term_a, term_b, dp_size)
    grad_a = grad_a.reshape(-1, rank, attention_columns)
    grad_b = grad_b.reshape(-1, rank, width_columns)

    wide = spread(chosen, out_b)
    contribution = lax.dot_general(
        wide, input_rows, (((0,), (0,)), ((), ())), preferred_element_type=jnp.float32
    )
    frozen = lax.dot_general(
        full_gradient, output_projection_weight, row_dims, preferred_element_type=jnp.float32
    )
    attention_gradient = (frozen + ADAPTER_SCALE * contribution).astype(jnp.bfloat16)
    return attention_gradient, grad_a, grad_b


def dot(a, b, dims):
    return lax.dot_general(a, b, dims, preferred_element_type=jnp.float32)


def kernel_call(body, **kwargs):
    return pl.pallas_call(
        body,
        compiler_params=pltpu.CompilerParams(vmem_limit_bytes=62 << 20),
        cost_estimate=pl.CostEstimate(flops=1 << 20, bytes_accessed=1 << 16, transcendentals=0),
        **kwargs,
    )


def together(*arrays):
    return lax.optimization_barrier(arrays)


def whole(array):
    return pl.BlockSpec(array.shape, lambda i, *_: (0,) * array.ndim)


def low_rank_kernel(rank, _, index_ref, down_ref, values_ref, up_ref, gradient_ref, out_ref):
    rows, tokens = down_ref.shape[0], values_ref.shape[0]
    step = pl.program_id(0)

    @pl.when(step == 0)
    def _():
        out_ref[...] = jnp.zeros_like(out_ref)

    adapter = lax.broadcasted_iota(jnp.int32, (rows // rank, 1, tokens), 0) + step * (rows // rank)
    chosen = adapter == index_ref[...][None]
    for at, weight, values in ((0, down_ref, values_ref), (rank, up_ref, gradient_ref)):
        terms = dot(weight[...], values[...], LAST).reshape(rows // rank, rank, tokens)
        out_ref[at : at + rank] += jnp.sum(jnp.where(chosen, terms, 0.0), axis=0)


def low_rank(after, index, down, values, up, gradient, rank):
    tokens = values.shape[0]
    rows = down.shape[0]
    block = rows // 4
    return kernel_call(
        functools.partial(low_rank_kernel, rank),
        grid=(4,),
        in_specs=[
            pl.BlockSpec(memory_space=pl.ANY),
            whole(index),
            pl.BlockSpec((block, down.shape[1]), lambda i: (i, 0)),
            whole(values),
            pl.BlockSpec((block, up.shape[1]), lambda i: (i, 0)),
            whole(gradient),
        ],
        out_specs=pl.BlockSpec((2 * rank, tokens), lambda i: (0, 0)),
        out_shape=jax.ShapeDtypeStruct((2 * rank, tokens), jnp.float32),
    )(after, index, down, values, up, gradient)


def spread_rows(labels, index, low):
    wide = jnp.concatenate([low] * (labels.shape[0] // low.shape[0]), axis=0)
    return jnp.where(labels == index, wide, 0.0).astype(jnp.bfloat16)


def adapter_gradient_kernel(
    here_ref, slots_ref, index_ref, pair, crossed, from_middle, values_ref, gradient_ref, send_ref, keep_ref, low_ref
):
    step = pl.program_id(0)

    @pl.when(step == 0)
    def _():
        middle = (here_ref[0] == 1) | (here_ref[0] == 2)
        total = pair[...] + crossed[...]
        low_ref[...] = jnp.where(middle, total, from_middle[...])

    rank = low_ref.shape[0] // 2
    low = low_ref[...].astype(jnp.bfloat16).astype(jnp.float32)
    multiplier = ADAPTER_SCALE * OBJECTIVE_WEIGHT
    a = multiplier * dot(
        spread_rows(slots_ref[...], index_ref[...], low[rank:]), values_ref[...], PLAIN
    )
    b = multiplier * dot(
        spread_rows(slots_ref[...], index_ref[...], low[:rank]), gradient_ref[...], PLAIN
    )
    split = a.shape[1]

    @pl.when(step < 2)
    def _():
        send_ref[:, :split] = a
        send_ref[:, split:] = b

    @pl.when(step >= 2)
    def _():
        keep_ref[:, :split] = a
        keep_ref[:, split:] = b


def adapter_gradients(here, slots, index, low_terms, values, gradient):
    rows = slots.shape[0]
    block = rows // 4
    width = values.shape[1] + gradient.shape[1]
    half = jax.ShapeDtypeStruct((rows // 2, width), jnp.float32)
    low = jax.ShapeDtypeStruct(low_terms[0].shape, jnp.float32)
    return kernel_call(
        adapter_gradient_kernel,
        grid_spec=pltpu.PrefetchScalarGridSpec(
            num_scalar_prefetch=1,
            grid=(4,),
            in_specs=[
                pl.BlockSpec((block, 1), lambda i, _: (i, 0)),
                whole(index),
                *(whole(term) for term in low_terms),
                whole(values),
                whole(gradient),
            ],
            out_specs=[
                pl.BlockSpec((block, width), lambda i, _: (jnp.minimum(i, 1), 0)),
                pl.BlockSpec((block, width), lambda i, _: (jnp.maximum(i - 2, 0), 0)),
                whole(low),
            ],
        ),
        out_shape=[half, half, low],
    )(here, slots, index, *low_terms, values, gradient)


def halves_kernel(keep_ref, got_ref, send_ref, out_ref):
    total = keep_ref[...] + got_ref[...]

    @pl.when(pl.program_id(0) < 2)
    def _():
        send_ref[...] = total.astype(send_ref.dtype)

    @pl.when(pl.program_id(0) >= 2)
    def _():
        out_ref[...] = total


def add_in_halves(keep, got):
    rows, width = keep.shape
    block = rows // 4
    both = pl.BlockSpec((block, width), lambda i: (i, 0))
    return kernel_call(
        halves_kernel,
        grid=(4,),
        in_specs=[both, both],
        out_specs=[
            pl.BlockSpec((block, width), lambda i: (jnp.minimum(i, 1), 0)),
            pl.BlockSpec((block, width), lambda i: (jnp.maximum(i - 2, 0), 0)),
        ],
        out_shape=[
            jax.ShapeDtypeStruct((rows // 2, width), jnp.bfloat16),
            jax.ShapeDtypeStruct((rows // 2, width), jnp.float32),
        ],
    )(keep, got)


def owned_kernel(keep_ref, got_ref, a_ref, b_ref):
    split = a_ref.shape[1]
    a_ref[...] = keep_ref[:, :split] + got_ref[:, :split].astype(jnp.float32)
    b_ref[...] = keep_ref[:, split:] + got_ref[:, split:].astype(jnp.float32)


def owned_sums(keep, got, split):
    rows, width = keep.shape
    block = rows // 4
    widths = (split, width - split)
    return kernel_call(
        owned_kernel,
        grid=(4,),
        in_specs=[pl.BlockSpec((block, width), lambda i: (i, 0))] * 2,
        out_specs=[pl.BlockSpec((block, w), lambda i: (i, 0)) for w in widths],
        out_shape=[jax.ShapeDtypeStruct((rows, w), jnp.float32) for w in widths],
    )(keep, got)


def rows_kernel(distances, first, here_ref, _, *refs):
    with_adapters = first is not None
    start_count = 3 if with_adapters else 1
    start_refs, refs = refs[:start_count], refs[start_count:]
    arrays, (weight_ref, out_ref, *scratch) = refs[: len(distances)], refs[len(distances) :]
    if with_adapters:
        index_ref, low_ref, rows_ref = start_refs
        (wide_ref,) = scratch

        @pl.when(pl.program_id(0) == 0)
        def _():
            rank = low_ref.shape[0] // 2
            labels = lax.broadcasted_iota(jnp.int32, wide_ref.shape[::-1], 0) // rank
            here_tokens = pl.ds(first, wide_ref.shape[0])
            low = low_ref[rank:, here_tokens].astype(jnp.bfloat16).astype(jnp.float32)
            wide_ref[...] = spread_rows(labels, index_ref[:, here_tokens], low).T

        total = ADAPTER_SCALE * dot(wide_ref[...], rows_ref[...], PLAIN)
    else:
        total = start_refs[0][...]
    columns = arrays[0].shape[1]
    blocks = {}
    for distance, ref in zip(distances, arrays):
        blocks[distance] = blocks[distance] + ref[...] if distance in blocks else ref[...]
    for distance, block in blocks.items():
        if weight_ref.shape[1] == columns:
            total += dot(block, weight_ref[...], LAST)
        else:
            at = pl.multiple_of((here_ref[0] ^ distance) * columns, 128)
            total += dot(block, weight_ref[:, pl.ds(at, columns)], LAST)
    out_ref[...] = total.astype(out_ref.dtype)


def add_products(here, before, start, blocks, weight, first, tokens, skip=0):
    step = blocks[-1][1].shape[0]
    features, width = weight.shape
    block = 1024 if len(blocks) == 2 else 512
    if before is None:
        out = jax.ShapeDtypeStruct((step, features), jnp.float32)
        out_block = pl.BlockSpec((step, block), lambda i, _: (0, i))
    elif first == 0:
        out = jax.ShapeDtypeStruct((tokens, features), jnp.bfloat16)
        out_block = pl.BlockSpec((step, block), lambda i, _: (0, i))
    else:
        out = jax.ShapeDtypeStruct((tokens, features), jnp.bfloat16)
        out_block = pl.BlockSpec(
            (pl.Element(step), pl.Element(block)), lambda i, _: (first, i * block)
        )
    distances, arrays = zip(*blocks)
    if len(set(distances)) == 1:
        weight_block = pl.BlockSpec(
            (block, arrays[0].shape[1]), lambda i, here: (i, here[0] ^ distances[0])
        )
    else:
        weight_block = pl.BlockSpec((block, width), lambda i, _: (i, 0))
    with_adapters = isinstance(start, tuple)
    if with_adapters:
        index, low, rows = start
        start_blocks = [
            whole(index),
            whole(low),
            pl.BlockSpec((rows.shape[0], block), lambda i, _: (0, i)),
        ]
        scratch = [pltpu.VMEM((step, rows.shape[0]), jnp.bfloat16)]
    else:
        start = (start,)
        start_blocks = [
            pl.BlockSpec((pl.Element(step), pl.Element(block)), lambda i, _: (skip, i * block))
        ]
        scratch = []
    return kernel_call(
        functools.partial(rows_kernel, distances, first if with_adapters else None),
        grid_spec=pltpu.PrefetchScalarGridSpec(
            num_scalar_prefetch=1,
            grid=(features // block,),
            in_specs=[
                pl.BlockSpec(memory_space=pl.ANY),
                *start_blocks,
                *(
                    pl.BlockSpec(
                        (pl.Element(step), pl.Element(b.shape[1])),
                        lambda i, _, b=b: (skip if b.shape[0] > step else 0, 0),
                    )
                    for b in arrays
                ),
                weight_block,
            ],
            out_specs=out_block,
            scratch_shapes=scratch,
        ),
        out_shape=out,
        input_output_aliases={} if before is None or before is here else {1: 0},
    )(here, here if before is None else before, *start, *arrays, weight)


def line_device(
    attention_output,
    projection_output_gradient,
    token_adapter_index,
    owner_slot_adapter,
    output_projection_weight,
    adapter_down_weight,
    adapter_up_weight,
):
    adapters, rank, attention_columns = adapter_down_weight.shape
    columns = adapter_up_weight.shape[2]
    tokens = attention_output.shape[0]
    here = lax.axis_index("tensor")[None]
    down = adapter_down_weight.reshape(adapters * rank, attention_columns)
    up = adapter_up_weight.reshape(adapters * rank, columns)
    index = token_adapter_index[None, :]

    cut = tokens * FIRST_EIGHTHS // 8
    order = jnp.array([3, 1, 2, 0], jnp.int32) ^ lax.axis_index("dp")
    slots = jnp.repeat(owner_slot_adapter.reshape(4, -1)[order].reshape(-1), rank)[:, None]
    weight = output_projection_weight

    def swap(block):
        return lax.ppermute(block, "tensor", pairs(4, 1))

    def cross(block):
        return lax.ppermute(block, "tensor", MIDDLES)

    def to_end(block):
        return lax.ppermute(block, "tensor", TO_ENDS)

    own = [projection_output_gradient[:cut], projection_output_gradient[cut:]]
    near, across, far, end_across, end_far = ({} for _ in range(5))

    near[0], across[0] = swap(own[0]), cross(own[0])
    low_part = low_rank(index, index, down, attention_output, up, projection_output_gradient, rank)
    low_near = swap(low_part)
    own_first, own_rest = own[1][:PIECE], own[1][PIECE:]
    near[0], across[0], low_near, own_first = together(near[0], across[0], low_near, own_first)
    near_first = swap(own_first)
    pair = low_part + low_near
    crossed = cross(pair)
    pair, crossed, near[0] = together(pair, crossed, near[0])
    from_middle = to_end(pair + crossed)
    near_first, from_middle, own_rest, near[0] = together(
        near_first, from_middle, own_rest, near[0]
    )
    near_rest, far[0] = swap(own_rest), cross(near[0])
    low_terms = (pair, crossed, from_middle)
    send, keep, low = adapter_gradients(
        here, slots, index, low_terms, attention_output, projection_output_gradient
    )
    send, keep, near_rest, far[0], across[0], own[1], index = together(
        send, keep, near_rest, far[0], across[0], own[1], index
    )
    near[1] = jnp.concatenate([near_first, near_rest], axis=0)
    end_across[0], across[1] = to_end(across[0]), cross(own[1])
    got = lax.ppermute(send, "dp", pairs(4, FLIP_CORE))
    end_far[0], far[1] = to_end(far[0]), cross(near[1])
    to_x, keep = add_in_halves(keep, got)
    to_x, keep, end_across[0], across[1], index = together(
        to_x, keep, end_across[0], across[1], index
    )
    got = lax.ppermute(to_x, "dp", pairs(4, FLIP_X))
    end_across[1] = to_end(across[1])
    base0 = add_products(
        here,
        None,
        (index, low, down),
        ((0, own[0]), (1, near[0]), (2, far[0]), (2, end_across[0])),
        weight,
        0,
        tokens,
    )
    base0, end_far[0] = together(base0, end_far[0])
    result = add_products(
        here, here, base0, ((3, across[0]), (3, end_far[0])), weight, 0, tokens
    )
    result, far[1], index = together(result, far[1], index)
    tail = far[1].shape[0] - LAST_ROWS
    end_far[1], end_far[2] = to_end(far[1][:tail]), to_end(far[1][tail:])
    grad_a, grad_b = owned_sums(keep, got, attention_columns)
    grad_a, grad_b, end_across[1], index = together(grad_a, grad_b, end_across[1], index)
    base = add_products(
        here,
        None,
        (index, low, down),
        ((0, own[1]), (1, near[1]), (2, far[1]), (2, end_across[1])),
        weight,
        cut,
        tokens,
    )
    base, end_far[1], result = together(base, end_far[1], result)
    result = add_products(
        here, result, base, ((3, across[1]), (3, end_far[1])), weight, cut, tokens
    )
    result, end_far[2] = together(result, end_far[2])
    result = add_products(
        here, result, base, ((3, across[1]), (3, end_far[2])), weight, cut + tail, tokens, tail
    )
    grad_a = grad_a.reshape(-1, rank, attention_columns)
    grad_b = grad_b.reshape(-1, rank, columns)
    return result, grad_a, grad_b


def per_device(*arrays):
    sizes = tuple(lax.axis_size(a) for a in ("parts", "tensor", "dp"))
    tokens, attention_columns = arrays[0].shape
    columns = arrays[1].shape[1]
    fits = tokens % 1024 == 0 and attention_columns % 2048 == 0 and columns % 128 == 0
    if sizes == (2, 4, 4) and fits:
        return line_device(*arrays)
    return general_device(*arrays)


def solution(mesh):
    placed = (
        P(("parts", "dp"), "tensor"),
        P(("parts", "dp"), "tensor"),
        P(("parts", "dp")),
        P(),
        P("tensor", None),
        P(None, None, "tensor"),
        P(None, None, "tensor"),
    )
    return jax.shard_map(
        per_device,
        mesh=mesh,
        in_specs=placed,
        out_specs=(
            P(("parts", "dp"), "tensor"),
            P(("parts", "dp"), None, "tensor"),
            P(("parts", "dp"), None, "tensor"),
        ),
        check_vma=False,
    )
```

```python
import functools

import jax
import jax.numpy as jnp
from jax import lax
from jax.experimental import pallas as pl
from jax.experimental.pallas import tpu as pltpu
from jax.sharding import PartitionSpec as P

ADAPTER_SCALE = 2.0
OBJECTIVE_WEIGHT = 0.05
LAST_ROWS = 256
PIECE = 160
FIRST_EIGHTHS = 3

TO_ENDS = [(1, 0), (2, 3)]
MIDDLES = [(1, 2), (2, 1)]
FLIP_X, FLIP_CORE = 2, 1
LAST = (((1,), (1,)), ((), ()))
FIRST = (((0,), (0,)), ((), ()))
PLAIN = (((1,), (0,)), ((), ()))


def pairs(size, distance):
    return [(i, i ^ distance) for i in range(size)]


def power_of_two(size):
    return size & (size - 1) == 0


def low_rank_part(rows, values, chosen):
    adapters, tokens = chosen.shape
    terms = lax.dot_general(
        rows, values, (((1,), (1,)), ((), ())), preferred_element_type=jnp.float32
    )
    terms = terms.reshape(adapters, -1, tokens)
    return jnp.sum(jnp.where(chosen[:, None, :], terms, jnp.zeros((), jnp.float32)), axis=0)


def spread(chosen, low):
    adapters, tokens = chosen.shape
    wide = jnp.where(chosen[:, None, :], low[None], jnp.zeros((), low.dtype))
    return wide.reshape(adapters * low.shape[0], tokens)


def sum_over_tensor(part, size):
    if not power_of_two(size) or size > 4:
        return lax.psum(part, "tensor")
    terms = [part] + [lax.ppermute(part, "tensor", pairs(size, d)) for d in range(1, size)]
    while len(terms) > 1:
        terms = [terms[i] + terms[i + 1] for i in range(0, len(terms), 2)]
    return terms[0]


def reduce_to_owner(term_a, term_b, size):
    if size != 4:
        return tuple(
            lax.psum_scatter(t, "dp", scatter_dimension=0, tiled=True) for t in (term_a, term_b)
        )
    for distance in (1, 2):
        half = term_a.shape[0] // 2
        got_a = lax.ppermute(term_a[:half], "dp", pairs(size, distance))
        got_b = lax.ppermute(term_b[:half], "dp", pairs(size, distance))
        term_a = term_a[half:] + got_a
        term_b = term_b[half:] + got_b
    return term_a, term_b


def general_device(
    attention_output,
    projection_output_gradient,
    token_adapter_index,
    owner_slot_adapter,
    output_projection_weight,
    adapter_down_weight,
    adapter_up_weight,
):
    adapters, rank, attention_columns = adapter_down_weight.shape
    width_columns = adapter_up_weight.shape[2]
    tokens = attention_output.shape[0]
    tensor_size = lax.axis_size("tensor")
    dp_size = lax.axis_size("dp")
    input_rows = adapter_down_weight.reshape(adapters * rank, attention_columns)
    output_rows = adapter_up_weight.reshape(adapters * rank, width_columns)
    labels = jnp.arange(adapters, dtype=jnp.int32)
    chosen = labels[:, None] == token_adapter_index[None, :]
    row_dims = (((1,), (1,)), ((), ()))

    full_gradient = lax.all_gather(projection_output_gradient, "tensor", axis=1, tiled=True)

    out_part = low_rank_part(output_rows, projection_output_gradient, chosen)
    in_part = low_rank_part(input_rows, attention_output, chosen)
    low = sum_over_tensor(jnp.concatenate([in_part, out_part], axis=0), tensor_size)
    low_b = low.astype(jnp.bfloat16)
    in_b, out_b = low_b[:rank], low_b[rank:]

    if dp_size == 4:
        order = jnp.array([3, 1, 2, 0], jnp.int32) ^ lax.axis_index("dp")
        slots = owner_slot_adapter.reshape(dp_size, -1)[order].reshape(-1)
    else:
        slots = owner_slot_adapter
    owned = slots[:, None] == token_adapter_index[None, :]
    multiplier = ADAPTER_SCALE * OBJECTIVE_WEIGHT
    term_a = multiplier * jnp.dot(
        spread(owned, out_b), attention_output, preferred_element_type=jnp.float32
    )
    term_b = multiplier * jnp.dot(
        spread(owned, in_b), projection_output_gradient, preferred_element_type=jnp.float32
    )
    grad_a, grad_b = reduce_to_owner(term_a, term_b, dp_size)
    grad_a = grad_a.reshape(-1, rank, attention_columns)
    grad_b = grad_b.reshape(-1, rank, width_columns)

    wide = spread(chosen, out_b)
    contribution = lax.dot_general(
        wide, input_rows, (((0,), (0,)), ((), ())), preferred_element_type=jnp.float32
    )
    frozen = lax.dot_general(
        full_gradient, output_projection_weight, row_dims, preferred_element_type=jnp.float32
    )
    attention_gradient = (frozen + ADAPTER_SCALE * contribution).astype(jnp.bfloat16)
    return attention_gradient, grad_a, grad_b


def dot(a, b, dims):
    return lax.dot_general(a, b, dims, preferred_element_type=jnp.float32)


def kernel_call(body, **kwargs):
    return pl.pallas_call(
        body,
        compiler_params=pltpu.CompilerParams(vmem_limit_bytes=62 << 20),
        cost_estimate=pl.CostEstimate(flops=1 << 20, bytes_accessed=1 << 16, transcendentals=0),
        **kwargs,
    )


def together(*arrays):
    return lax.optimization_barrier(arrays)


def whole(array):
    return pl.BlockSpec(array.shape, lambda i, *_: (0,) * array.ndim)


def low_rank_kernel(rank, _, index_ref, down_ref, values_ref, up_ref, gradient_ref, out_ref):
    rows, tokens = down_ref.shape[0], values_ref.shape[0]
    step = pl.program_id(0)

    @pl.when(step == 0)
    def _():
        out_ref[...] = jnp.zeros_like(out_ref)

    adapter = lax.broadcasted_iota(jnp.int32, (rows // rank, 1, tokens), 0) + step * (rows // rank)
    chosen = adapter == index_ref[...][None]
    for at, weight, values in ((0, down_ref, values_ref), (rank, up_ref, gradient_ref)):
        terms = dot(weight[...], values[...], LAST).reshape(rows // rank, rank, tokens)
        out_ref[at : at + rank] += jnp.sum(jnp.where(chosen, terms, 0.0), axis=0)


def low_rank(after, index, down, values, up, gradient, rank):
    tokens = values.shape[0]
    rows = down.shape[0]
    block = rows // 4
    return kernel_call(
        functools.partial(low_rank_kernel, rank),
        grid=(4,),
        in_specs=[
            pl.BlockSpec(memory_space=pl.ANY),
            whole(index),
            pl.BlockSpec((block, down.shape[1]), lambda i: (i, 0)),
            whole(values),
            pl.BlockSpec((block, up.shape[1]), lambda i: (i, 0)),
            whole(gradient),
        ],
        out_specs=pl.BlockSpec((2 * rank, tokens), lambda i: (0, 0)),
        out_shape=jax.ShapeDtypeStruct((2 * rank, tokens), jnp.float32),
    )(after, index, down, values, up, gradient)


def spread_rows(labels, index, low):
    wide = jnp.concatenate([low] * (labels.shape[0] // low.shape[0]), axis=0)
    return jnp.where(labels == index, wide, 0.0).astype(jnp.bfloat16)


def adapter_gradient_kernel(
    here_ref, slots_ref, index_ref, pair, crossed, from_middle, values_ref, gradient_ref, send_ref, keep_ref, low_ref
):
    step = pl.program_id(0)

    @pl.when(step == 0)
    def _():
        middle = (here_ref[0] == 1) | (here_ref[0] == 2)
        total = pair[...] + crossed[...]
        low_ref[...] = jnp.where(middle, total, from_middle[...])

    rank = low_ref.shape[0] // 2
    low = low_ref[...].astype(jnp.bfloat16).astype(jnp.float32)
    multiplier = ADAPTER_SCALE * OBJECTIVE_WEIGHT
    a = multiplier * dot(
        spread_rows(slots_ref[...], index_ref[...], low[rank:]), values_ref[...], PLAIN
    )
    b = multiplier * dot(
        spread_rows(slots_ref[...], index_ref[...], low[:rank]), gradient_ref[...], PLAIN
    )
    split = a.shape[1]

    @pl.when(step < 2)
    def _():
        send_ref[:, :split] = a
        send_ref[:, split:] = b

    @pl.when(step >= 2)
    def _():
        keep_ref[:, :split] = a
        keep_ref[:, split:] = b


def adapter_gradients(here, slots, index, low_terms, values, gradient):
    rows = slots.shape[0]
    block = rows // 4
    width = values.shape[1] + gradient.shape[1]
    half = jax.ShapeDtypeStruct((rows // 2, width), jnp.float32)
    low = jax.ShapeDtypeStruct(low_terms[0].shape, jnp.float32)
    return kernel_call(
        adapter_gradient_kernel,
        grid_spec=pltpu.PrefetchScalarGridSpec(
            num_scalar_prefetch=1,
            grid=(4,),
            in_specs=[
                pl.BlockSpec((block, 1), lambda i, _: (i, 0)),
                whole(index),
                *(whole(term) for term in low_terms),
                whole(values),
                whole(gradient),
            ],
            out_specs=[
                pl.BlockSpec((block, width), lambda i, _: (jnp.minimum(i, 1), 0)),
                pl.BlockSpec((block, width), lambda i, _: (jnp.maximum(i - 2, 0), 0)),
                whole(low),
            ],
        ),
        out_shape=[half, half, low],
    )(here, slots, index, *low_terms, values, gradient)


def halves_kernel(keep_ref, got_ref, send_ref, out_ref):
    total = keep_ref[...] + got_ref[...]

    @pl.when(pl.program_id(0) < 2)
    def _():
        send_ref[...] = total.astype(send_ref.dtype)

    @pl.when(pl.program_id(0) >= 2)
    def _():
        out_ref[...] = total


def add_in_halves(keep, got):
    rows, width = keep.shape
    block = rows // 4
    both = pl.BlockSpec((block, width), lambda i: (i, 0))
    return kernel_call(
        halves_kernel,
        grid=(4,),
        in_specs=[both, both],
        out_specs=[
            pl.BlockSpec((block, width), lambda i: (jnp.minimum(i, 1), 0)),
            pl.BlockSpec((block, width), lambda i: (jnp.maximum(i - 2, 0), 0)),
        ],
        out_shape=[
            jax.ShapeDtypeStruct((rows // 2, width), jnp.bfloat16),
            jax.ShapeDtypeStruct((rows // 2, width), jnp.float32),
        ],
    )(keep, got)


def owned_kernel(keep_ref, got_ref, a_ref, b_ref):
    split = a_ref.shape[1]
    a_ref[...] = keep_ref[:, :split] + got_ref[:, :split].astype(jnp.float32)
    b_ref[...] = keep_ref[:, split:] + got_ref[:, split:].astype(jnp.float32)


def owned_sums(keep, got, split):
    rows, width = keep.shape
    block = rows // 4
    widths = (split, width - split)
    return kernel_call(
        owned_kernel,
        grid=(4,),
        in_specs=[pl.BlockSpec((block, width), lambda i: (i, 0))] * 2,
        out_specs=[pl.BlockSpec((block, w), lambda i: (i, 0)) for w in widths],
        out_shape=[jax.ShapeDtypeStruct((rows, w), jnp.float32) for w in widths],
    )(keep, got)


def rows_kernel(distances, first, here_ref, _, *refs):
    with_adapters = first is not None
    start_count = 3 if with_adapters else 1
    start_refs, refs = refs[:start_count], refs[start_count:]
    arrays, (weight_ref, out_ref, *scratch) = refs[: len(distances)], refs[len(distances) :]
    if with_adapters:
        index_ref, low_ref, rows_ref = start_refs
        (wide_ref,) = scratch

        @pl.when(pl.program_id(0) == 0)
        def _():
            rank = low_ref.shape[0] // 2
            labels = lax.broadcasted_iota(jnp.int32, wide_ref.shape[::-1], 0) // rank
            here_tokens = pl.ds(first, wide_ref.shape[0])
            low = low_ref[rank:, here_tokens].astype(jnp.bfloat16).astype(jnp.float32)
            wide_ref[...] = spread_rows(labels, index_ref[:, here_tokens], low).T

        total = ADAPTER_SCALE * dot(wide_ref[...], rows_ref[...], PLAIN)
    else:
        total = start_refs[0][...]
    columns = arrays[0].shape[1]
    blocks = {}
    for distance, ref in zip(distances, arrays):
        blocks[distance] = blocks[distance] + ref[...] if distance in blocks else ref[...]
    for distance, block in blocks.items():
        if weight_ref.shape[1] == columns:
            total += dot(block, weight_ref[...], LAST)
        else:
            at = pl.multiple_of((here_ref[0] ^ distance) * columns, 128)
            total += dot(block, weight_ref[:, pl.ds(at, columns)], LAST)
    out_ref[...] = total.astype(out_ref.dtype)


def add_products(here, before, start, blocks, weight, first, tokens, skip=0):
    step = blocks[-1][1].shape[0]
    features, width = weight.shape
    block = 1024 if len(blocks) == 2 else 512
    if before is None:
        out = jax.ShapeDtypeStruct((step, features), jnp.float32)
        out_block = pl.BlockSpec((step, block), lambda i, _: (0, i))
    elif first == 0:
        out = jax.ShapeDtypeStruct((tokens, features), jnp.bfloat16)
        out_block = pl.BlockSpec((step, block), lambda i, _: (0, i))
    else:
        out = jax.ShapeDtypeStruct((tokens, features), jnp.bfloat16)
        out_block = pl.BlockSpec(
            (pl.Element(step), pl.Element(block)), lambda i, _: (first, i * block)
        )
    distances, arrays = zip(*blocks)
    if len(set(distances)) == 1:
        weight_block = pl.BlockSpec(
            (block, arrays[0].shape[1]), lambda i, here: (i, here[0] ^ distances[0])
        )
    else:
        weight_block = pl.BlockSpec((block, width), lambda i, _: (i, 0))
    with_adapters = isinstance(start, tuple)
    if with_adapters:
        index, low, rows = start
        start_blocks = [
            whole(index),
            whole(low),
            pl.BlockSpec((rows.shape[0], block), lambda i, _: (0, i)),
        ]
        scratch = [pltpu.VMEM((step, rows.shape[0]), jnp.bfloat16)]
    else:
        start = (start,)
        start_blocks = [
            pl.BlockSpec((pl.Element(step), pl.Element(block)), lambda i, _: (skip, i * block))
        ]
        scratch = []
    return kernel_call(
        functools.partial(rows_kernel, distances, first if with_adapters else None),
        grid_spec=pltpu.PrefetchScalarGridSpec(
            num_scalar_prefetch=1,
            grid=(features // block,),
            in_specs=[
                pl.BlockSpec(memory_space=pl.ANY),
                *start_blocks,
                *(
                    pl.BlockSpec(
                        (pl.Element(step), pl.Element(b.shape[1])),
                        lambda i, _, b=b: (skip if b.shape[0] > step else 0, 0),
                    )
                    for b in arrays
                ),
                weight_block,
            ],
            out_specs=out_block,
            scratch_shapes=scratch,
        ),
        out_shape=out,
        input_output_aliases={} if before is None or before is here else {1: 0},
    )(here, here if before is None else before, *start, *arrays, weight)


def line_device(
    attention_output,
    projection_output_gradient,
    token_adapter_index,
    owner_slot_adapter,
    output_projection_weight,
    adapter_down_weight,
    adapter_up_weight,
):
    adapters, rank, attention_columns = adapter_down_weight.shape
    columns = adapter_up_weight.shape[2]
    tokens = attention_output.shape[0]
    here = lax.axis_index("tensor")[None]
    down = adapter_down_weight.reshape(adapters * rank, attention_columns)
    up = adapter_up_weight.reshape(adapters * rank, columns)
    index = token_adapter_index[None, :]

    cut = tokens * FIRST_EIGHTHS // 8
    order = jnp.array([3, 1, 2, 0], jnp.int32) ^ lax.axis_index("dp")
    slots = jnp.repeat(owner_slot_adapter.reshape(4, -1)[order].reshape(-1), rank)[:, None]
    weight = output_projection_weight

    def swap(block):
        return lax.ppermute(block, "tensor", pairs(4, 1))

    def cross(block):
        return lax.ppermute(block, "tensor", MIDDLES)

    def to_end(block):
        return lax.ppermute(block, "tensor", TO_ENDS)

    own = [projection_output_gradient[:cut], projection_output_gradient[cut:]]
    near, across, far, end_across, end_far = ({} for _ in range(5))

    near[0], across[0] = swap(own[0]), cross(own[0])
    low_part = low_rank(index, index, down, attention_output, up, projection_output_gradient, rank)
    low_near = swap(low_part)
    own_first, own_rest = own[1][:PIECE], own[1][PIECE:]
    near[0], across[0], low_near, own_first = together(near[0], across[0], low_near, own_first)
    near_first = swap(own_first)
    pair = low_part + low_near
    crossed = cross(pair)
    pair, crossed, near[0] = together(pair, crossed, near[0])
    from_middle = to_end(pair + crossed)
    near_first, from_middle, own_rest, near[0] = together(
        near_first, from_middle, own_rest, near[0]
    )
    near_rest, far[0] = swap(own_rest), cross(near[0])
    low_terms = (pair, crossed, from_middle)
    send, keep, low = adapter_gradients(
        here, slots, index, low_terms, attention_output, projection_output_gradient
    )
    send, keep, near_rest, far[0], across[0], own[1], index = together(
        send, keep, near_rest, far[0], across[0], own[1], index
    )
    near[1] = jnp.concatenate([near_first, near_rest], axis=0)
    end_across[0], across[1] = to_end(across[0]), cross(own[1])
    got = lax.ppermute(send, "dp", pairs(4, FLIP_CORE))
    end_far[0], far[1] = to_end(far[0]), cross(near[1])
    to_x, keep = add_in_halves(keep, got)
    to_x, keep, end_across[0], across[1], index = together(
        to_x, keep, end_across[0], across[1], index
    )
    got = lax.ppermute(to_x, "dp", pairs(4, FLIP_X))
    end_across[1] = to_end(across[1])
    base0 = add_products(
        here,
        None,
        (index, low, down),
        ((0, own[0]), (1, near[0]), (2, far[0]), (2, end_across[0])),
        weight,
        0,
        tokens,
    )
    base0, end_far[0] = together(base0, end_far[0])
    result = add_products(
        here, here, base0, ((3, across[0]), (3, end_far[0])), weight, 0, tokens
    )
    result, far[1], index = together(result, far[1], index)
    tail = far[1].shape[0] - LAST_ROWS
    end_far[1], end_far[2] = to_end(far[1][:tail]), to_end(far[1][tail:])
    grad_a, grad_b = owned_sums(keep, got, attention_columns)
    grad_a, grad_b, end_across[1], index = together(grad_a, grad_b, end_across[1], index)
    base = add_products(
        here,
        None,
        (index, low, down),
        ((0, own[1]), (1, near[1]), (2, far[1]), (2, end_across[1])),
        weight,
        cut,
        tokens,
    )
    base, end_far[1], result = together(base, end_far[1], result)
    result = add_products(
        here, result, base, ((3, across[1]), (3, end_far[1])), weight, cut, tokens
    )
    result, end_far[2] = together(result, end_far[2])
    result = add_products(
        here, result, base, ((3, across[1]), (3, end_far[2])), weight, cut + tail, tokens, tail
    )
    grad_a = grad_a.reshape(-1, rank, attention_columns)
    grad_b = grad_b.reshape(-1, rank, columns)
    return result, grad_a, grad_b


def per_device(*arrays):
    sizes = tuple(lax.axis_size(a) for a in ("parts", "tensor", "dp"))
    tokens, attention_columns = arrays[0].shape
    columns = arrays[1].shape[1]
    fits = tokens % 1024 == 0 and attention_columns % 2048 == 0 and columns % 128 == 0
    if sizes == (2, 4, 4) and fits:
        return line_device(*arrays)
    return general_device(*arrays)


def solution(mesh):
    placed = (
        P(("parts", "dp"), "tensor"),
        P(("parts", "dp"), "tensor"),
        P(("parts", "dp")),
        P(),
        P("tensor", None),
        P(None, None, "tensor"),
        P(None, None, "tensor"),
    )
    return jax.shard_map(
        per_device,
        mesh=mesh,
        in_specs=placed,
        out_specs=(
            P(("parts", "dp"), "tensor"),
            P(("parts", "dp"), None, "tensor"),
            P(("parts", "dp"), None, "tensor"),
        ),
        check_vma=False,
    )
```

```python
import functools

import jax
import jax.numpy as jnp
from jax import lax
from jax.experimental import pallas as pl
from jax.experimental.pallas import tpu as pltpu
from jax.sharding import PartitionSpec as P

ADAPTER_SCALE = 2.0
OBJECTIVE_WEIGHT = 0.05
LAST_ROWS = 256
PIECE = 160
FIRST_EIGHTHS = 3

TO_ENDS = [(1, 0), (2, 3)]
MIDDLES = [(1, 2), (2, 1)]
FLIP_X, FLIP_CORE = 2, 1
LAST = (((1,), (1,)), ((), ()))
FIRST = (((0,), (0,)), ((), ()))
PLAIN = (((1,), (0,)), ((), ()))


def pairs(size, distance):
    return [(i, i ^ distance) for i in range(size)]


def power_of_two(size):
    return size & (size - 1) == 0


def low_rank_part(rows, values, chosen):
    adapters, tokens = chosen.shape
    terms = lax.dot_general(
        rows, values, (((1,), (1,)), ((), ())), preferred_element_type=jnp.float32
    )
    terms = terms.reshape(adapters, -1, tokens)
    return jnp.sum(jnp.where(chosen[:, None, :], terms, jnp.zeros((), jnp.float32)), axis=0)


def spread(chosen, low):
    adapters, tokens = chosen.shape
    wide = jnp.where(chosen[:, None, :], low[None], jnp.zeros((), low.dtype))
    return wide.reshape(adapters * low.shape[0], tokens)


def sum_over_tensor(part, size):
    if not power_of_two(size) or size > 4:
        return lax.psum(part, "tensor")
    terms = [part] + [lax.ppermute(part, "tensor", pairs(size, d)) for d in range(1, size)]
    while len(terms) > 1:
        terms = [terms[i] + terms[i + 1] for i in range(0, len(terms), 2)]
    return terms[0]


def reduce_to_owner(term_a, term_b, size):
    if size != 4:
        return tuple(
            lax.psum_scatter(t, "dp", scatter_dimension=0, tiled=True) for t in (term_a, term_b)
        )
    for distance in (1, 2):
        half = term_a.shape[0] // 2
        got_a = lax.ppermute(term_a[:half], "dp", pairs(size, distance))
        got_b = lax.ppermute(term_b[:half], "dp", pairs(size, distance))
        term_a = term_a[half:] + got_a
        term_b = term_b[half:] + got_b
    return term_a, term_b


def general_device(
    attention_output,
    projection_output_gradient,
    token_adapter_index,
    owner_slot_adapter,
    output_projection_weight,
    adapter_down_weight,
    adapter_up_weight,
):
    adapters, rank, attention_columns = adapter_down_weight.shape
    width_columns = adapter_up_weight.shape[2]
    tokens = attention_output.shape[0]
    tensor_size = lax.axis_size("tensor")
    dp_size = lax.axis_size("dp")
    input_rows = adapter_down_weight.reshape(adapters * rank, attention_columns)
    output_rows = adapter_up_weight.reshape(adapters * rank, width_columns)
    labels = jnp.arange(adapters, dtype=jnp.int32)
    chosen = labels[:, None] == token_adapter_index[None, :]
    row_dims = (((1,), (1,)), ((), ()))

    full_gradient = lax.all_gather(projection_output_gradient, "tensor", axis=1, tiled=True)

    out_part = low_rank_part(output_rows, projection_output_gradient, chosen)
    in_part = low_rank_part(input_rows, attention_output, chosen)
    low = sum_over_tensor(jnp.concatenate([in_part, out_part], axis=0), tensor_size)
    low_b = low.astype(jnp.bfloat16)
    in_b, out_b = low_b[:rank], low_b[rank:]

    if dp_size == 4:
        order = jnp.array([3, 1, 2, 0], jnp.int32) ^ lax.axis_index("dp")
        slots = owner_slot_adapter.reshape(dp_size, -1)[order].reshape(-1)
    else:
        slots = owner_slot_adapter
    owned = slots[:, None] == token_adapter_index[None, :]
    multiplier = ADAPTER_SCALE * OBJECTIVE_WEIGHT
    term_a = multiplier * jnp.dot(
        spread(owned, out_b), attention_output, preferred_element_type=jnp.float32
    )
    term_b = multiplier * jnp.dot(
        spread(owned, in_b), projection_output_gradient, preferred_element_type=jnp.float32
    )
    grad_a, grad_b = reduce_to_owner(term_a, term_b, dp_size)
    grad_a = grad_a.reshape(-1, rank, attention_columns)
    grad_b = grad_b.reshape(-1, rank, width_columns)

    wide = spread(chosen, out_b)
    contribution = lax.dot_general(
        wide, input_rows, (((0,), (0,)), ((), ())), preferred_element_type=jnp.float32
    )
    frozen = lax.dot_general(
        full_gradient, output_projection_weight, row_dims, preferred_element_type=jnp.float32
    )
    attention_gradient = (frozen + ADAPTER_SCALE * contribution).astype(jnp.bfloat16)
    return attention_gradient, grad_a, grad_b


def dot(a, b, dims):
    return lax.dot_general(a, b, dims, preferred_element_type=jnp.float32)


def kernel_call(body, **kwargs):
    return pl.pallas_call(
        body,
        compiler_params=pltpu.CompilerParams(vmem_limit_bytes=62 << 20),
        cost_estimate=pl.CostEstimate(flops=1 << 20, bytes_accessed=1 << 16, transcendentals=0),
        **kwargs,
    )


def together(*arrays):
    return lax.optimization_barrier(arrays)


def whole(array):
    return pl.BlockSpec(array.shape, lambda i, *_: (0,) * array.ndim)


def low_rank_kernel(rank, _, index_ref, down_ref, values_ref, up_ref, gradient_ref, out_ref):
    rows, tokens = down_ref.shape[0], values_ref.shape[0]
    step = pl.program_id(0)

    @pl.when(step == 0)
    def _():
        out_ref[...] = jnp.zeros_like(out_ref)

    adapter = lax.broadcasted_iota(jnp.int32, (rows // rank, 1, tokens), 0) + step * (rows // rank)
    chosen = adapter == index_ref[...][None]
    for at, weight, values in ((0, down_ref, values_ref), (rank, up_ref, gradient_ref)):
        terms = dot(weight[...], values[...], LAST).reshape(rows // rank, rank, tokens)
        out_ref[at : at + rank] += jnp.sum(jnp.where(chosen, terms, 0.0), axis=0)


def low_rank(after, index, down, values, up, gradient, rank):
    tokens = values.shape[0]
    rows = down.shape[0]
    block = rows // 4
    return kernel_call(
        functools.partial(low_rank_kernel, rank),
        grid=(4,),
        in_specs=[
            pl.BlockSpec(memory_space=pl.ANY),
            whole(index),
            pl.BlockSpec((block, down.shape[1]), lambda i: (i, 0)),
            whole(values),
            pl.BlockSpec((block, up.shape[1]), lambda i: (i, 0)),
            whole(gradient),
        ],
        out_specs=pl.BlockSpec((2 * rank, tokens), lambda i: (0, 0)),
        out_shape=jax.ShapeDtypeStruct((2 * rank, tokens), jnp.float32),
    )(after, index, down, values, up, gradient)


def spread_rows(labels, index, low):
    wide = jnp.concatenate([low] * (labels.shape[0] // low.shape[0]), axis=0)
    return jnp.where(labels == index, wide, 0.0).astype(jnp.bfloat16)


def adapter_gradient_kernel(
    here_ref, slots_ref, index_ref, pair, crossed, from_middle, values_ref, gradient_ref, send_ref, keep_ref, low_ref
):
    step = pl.program_id(0)

    @pl.when(step == 0)
    def _():
        middle = (here_ref[0] == 1) | (here_ref[0] == 2)
        total = pair[...] + crossed[...]
        low_ref[...] = jnp.where(middle, total, from_middle[...])

    rank = low_ref.shape[0] // 2
    low = low_ref[...].astype(jnp.bfloat16).astype(jnp.float32)
    multiplier = ADAPTER_SCALE * OBJECTIVE_WEIGHT
    a = multiplier * dot(
        spread_rows(slots_ref[...], index_ref[...], low[rank:]), values_ref[...], PLAIN
    )
    b = multiplier * dot(
        spread_rows(slots_ref[...], index_ref[...], low[:rank]), gradient_ref[...], PLAIN
    )
    split = a.shape[1]

    @pl.when(step < 2)
    def _():
        send_ref[:, :split] = a
        send_ref[:, split:] = b

    @pl.when(step >= 2)
    def _():
        keep_ref[:, :split] = a
        keep_ref[:, split:] = b


def adapter_gradients(here, slots, index, low_terms, values, gradient):
    rows = slots.shape[0]
    block = rows // 4
    width = values.shape[1] + gradient.shape[1]
    half = jax.ShapeDtypeStruct((rows // 2, width), jnp.float32)
    low = jax.ShapeDtypeStruct(low_terms[0].shape, jnp.float32)
    return kernel_call(
        adapter_gradient_kernel,
        grid_spec=pltpu.PrefetchScalarGridSpec(
            num_scalar_prefetch=1,
            grid=(4,),
            in_specs=[
                pl.BlockSpec((block, 1), lambda i, _: (i, 0)),
                whole(index),
                *(whole(term) for term in low_terms),
                whole(values),
                whole(gradient),
            ],
            out_specs=[
                pl.BlockSpec((block, width), lambda i, _: (jnp.minimum(i, 1), 0)),
                pl.BlockSpec((block, width), lambda i, _: (jnp.maximum(i - 2, 0), 0)),
                whole(low),
            ],
        ),
        out_shape=[half, half, low],
    )(here, slots, index, *low_terms, values, gradient)


def halves_kernel(keep_ref, got_ref, send_ref, out_ref):
    total = keep_ref[...] + got_ref[...]

    @pl.when(pl.program_id(0) < 2)
    def _():
        send_ref[...] = total.astype(send_ref.dtype)

    @pl.when(pl.program_id(0) >= 2)
    def _():
        out_ref[...] = total


def add_in_halves(keep, got):
    rows, width = keep.shape
    block = rows // 4
    both = pl.BlockSpec((block, width), lambda i: (i, 0))
    return kernel_call(
        halves_kernel,
        grid=(4,),
        in_specs=[both, both],
        out_specs=[
            pl.BlockSpec((block, width), lambda i: (jnp.minimum(i, 1), 0)),
            pl.BlockSpec((block, width), lambda i: (jnp.maximum(i - 2, 0), 0)),
        ],
        out_shape=[
            jax.ShapeDtypeStruct((rows // 2, width), jnp.bfloat16),
            jax.ShapeDtypeStruct((rows // 2, width), jnp.float32),
        ],
    )(keep, got)


def owned_kernel(keep_ref, got_ref, a_ref, b_ref):
    split = a_ref.shape[1]
    a_ref[...] = keep_ref[:, :split] + got_ref[:, :split].astype(jnp.float32)
    b_ref[...] = keep_ref[:, split:] + got_ref[:, split:].astype(jnp.float32)


def owned_sums(keep, got, split):
    rows, width = keep.shape
    block = rows // 4
    widths = (split, width - split)
    return kernel_call(
        owned_kernel,
        grid=(4,),
        in_specs=[pl.BlockSpec((block, width), lambda i: (i, 0))] * 2,
        out_specs=[pl.BlockSpec((block, w), lambda i: (i, 0)) for w in widths],
        out_shape=[jax.ShapeDtypeStruct((rows, w), jnp.float32) for w in widths],
    )(keep, got)


def rows_kernel(distances, first, here_ref, _, *refs):
    with_adapters = first is not None
    start_count = 3 if with_adapters else 1
    start_refs, refs = refs[:start_count], refs[start_count:]
    arrays, (weight_ref, out_ref, *scratch) = refs[: len(distances)], refs[len(distances) :]
    if with_adapters:
        index_ref, low_ref, rows_ref = start_refs
        (wide_ref,) = scratch

        @pl.when(pl.program_id(0) == 0)
        def _():
            rank = low_ref.shape[0] // 2
            labels = lax.broadcasted_iota(jnp.int32, wide_ref.shape[::-1], 0) // rank
            here_tokens = pl.ds(first, wide_ref.shape[0])
            low = low_ref[rank:, here_tokens].astype(jnp.bfloat16).astype(jnp.float32)
            wide_ref[...] = spread_rows(labels, index_ref[:, here_tokens], low).T

        total = ADAPTER_SCALE * dot(wide_ref[...], rows_ref[...], PLAIN)
    else:
        total = start_refs[0][...]
    columns = arrays[0].shape[1]
    blocks = {}
    for distance, ref in zip(distances, arrays):
        blocks[distance] = blocks[distance] + ref[...] if distance in blocks else ref[...]
    for distance, block in blocks.items():
        if weight_ref.shape[1] == columns:
            total += dot(block, weight_ref[...], LAST)
        else:
            at = pl.multiple_of((here_ref[0] ^ distance) * columns, 128)
            total += dot(block, weight_ref[:, pl.ds(at, columns)], LAST)
    out_ref[...] = total.astype(out_ref.dtype)


def add_products(here, before, start, blocks, weight, first, tokens, skip=0):
    step = blocks[-1][1].shape[0]
    features, width = weight.shape
    block = 1024 if len(blocks) == 2 else 512
    if before is None:
        out = jax.ShapeDtypeStruct((step, features), jnp.float32)
        out_block = pl.BlockSpec((step, block), lambda i, _: (0, i))
    elif first == 0:
        out = jax.ShapeDtypeStruct((tokens, features), jnp.bfloat16)
        out_block = pl.BlockSpec((step, block), lambda i, _: (0, i))
    else:
        out = jax.ShapeDtypeStruct((tokens, features), jnp.bfloat16)
        out_block = pl.BlockSpec(
            (pl.Element(step), pl.Element(block)), lambda i, _: (first, i * block)
        )
    distances, arrays = zip(*blocks)
    if len(set(distances)) == 1:
        weight_block = pl.BlockSpec(
            (block, arrays[0].shape[1]), lambda i, here: (i, here[0] ^ distances[0])
        )
    else:
        weight_block = pl.BlockSpec((block, width), lambda i, _: (i, 0))
    with_adapters = isinstance(start, tuple)
    if with_adapters:
        index, low, rows = start
        start_blocks = [
            whole(index),
            whole(low),
            pl.BlockSpec((rows.shape[0], block), lambda i, _: (0, i)),
        ]
        scratch = [pltpu.VMEM((step, rows.shape[0]), jnp.bfloat16)]
    else:
        start = (start,)
        start_blocks = [
            pl.BlockSpec((pl.Element(step), pl.Element(block)), lambda i, _: (skip, i * block))
        ]
        scratch = []
    return kernel_call(
        functools.partial(rows_kernel, distances, first if with_adapters else None),
        grid_spec=pltpu.PrefetchScalarGridSpec(
            num_scalar_prefetch=1,
            grid=(features // block,),
            in_specs=[
                pl.BlockSpec(memory_space=pl.ANY),
                *start_blocks,
                *(
                    pl.BlockSpec(
                        (pl.Element(step), pl.Element(b.shape[1])),
                        lambda i, _, b=b: (skip if b.shape[0] > step else 0, 0),
                    )
                    for b in arrays
                ),
                weight_block,
            ],
            out_specs=out_block,
            scratch_shapes=scratch,
        ),
        out_shape=out,
        input_output_aliases={} if before is None or before is here else {1: 0},
    )(here, here if before is None else before, *start, *arrays, weight)


def line_device(
    attention_output,
    projection_output_gradient,
    token_adapter_index,
    owner_slot_adapter,
    output_projection_weight,
    adapter_down_weight,
    adapter_up_weight,
):
    adapters, rank, attention_columns = adapter_down_weight.shape
    columns = adapter_up_weight.shape[2]
    tokens = attention_output.shape[0]
    here = lax.axis_index("tensor")[None]
    down = adapter_down_weight.reshape(adapters * rank, attention_columns)
    up = adapter_up_weight.reshape(adapters * rank, columns)
    index = token_adapter_index[None, :]

    cut = tokens * FIRST_EIGHTHS // 8
    order = jnp.array([3, 1, 2, 0], jnp.int32) ^ lax.axis_index("dp")
    slots = jnp.repeat(owner_slot_adapter.reshape(4, -1)[order].reshape(-1), rank)[:, None]
    weight = output_projection_weight

    def swap(block):
        return lax.ppermute(block, "tensor", pairs(4, 1))

    def cross(block):
        return lax.ppermute(block, "tensor", MIDDLES)

    def to_end(block):
        return lax.ppermute(block, "tensor", TO_ENDS)

    own = [projection_output_gradient[:cut], projection_output_gradient[cut:]]
    near, across, far, end_across, end_far = ({} for _ in range(5))

    near[0], across[0] = swap(own[0]), cross(own[0])
    low_part = low_rank(index, index, down, attention_output, up, projection_output_gradient, rank)
    low_near = swap(low_part)
    own_first, own_rest = own[1][:PIECE], own[1][PIECE:]
    near[0], across[0], low_near, own_first = together(near[0], across[0], low_near, own_first)
    near_first = swap(own_first)
    pair = low_part + low_near
    crossed = cross(pair)
    pair, crossed, near[0] = together(pair, crossed, near[0])
    from_middle = to_end(pair + crossed)
    near_first, from_middle, own_rest, near[0] = together(
        near_first, from_middle, own_rest, near[0]
    )
    near_rest, far[0] = swap(own_rest), cross(near[0])
    low_terms = (pair, crossed, from_middle)
    send, keep, low = adapter_gradients(
        here, slots, index, low_terms, attention_output, projection_output_gradient
    )
    send, keep, near_rest, far[0], across[0], own[1], index = together(
        send, keep, near_rest, far[0], across[0], own[1], index
    )
    end_across[0], across[1] = to_end(across[0]), cross(own[1])
    got = lax.ppermute(send, "dp", pairs(4, FLIP_CORE))
    end_far[0] = to_end(far[0])
    got, near_first, near_rest = together(got, near_first, near_rest)
    near[1] = jnp.concatenate([near_first, near_rest], axis=0)
    far[1] = cross(near[1])
    to_x, keep = add_in_halves(keep, got)
    to_x, keep, end_across[0], across[1], index = together(
        to_x, keep, end_across[0], across[1], index
    )
    got = lax.ppermute(to_x, "dp", pairs(4, FLIP_X))
    end_across[1] = to_end(across[1])
    base0 = add_products(
        here,
        None,
        (index, low, down),
        ((0, own[0]), (1, near[0]), (2, far[0]), (2, end_across[0])),
        weight,
        0,
        tokens,
    )
    base0, end_far[0] = together(base0, end_far[0])
    result = add_products(
        here, here, base0, ((3, across[0]), (3, end_far[0])), weight, 0, tokens
    )
    result, far[1], index = together(result, far[1], index)
    tail = far[1].shape[0] - LAST_ROWS
    end_far[1], end_far[2] = to_end(far[1][:tail]), to_end(far[1][tail:])
    grad_a, grad_b = owned_sums(keep, got, attention_columns)
    grad_a, grad_b, end_across[1], index = together(grad_a, grad_b, end_across[1], index)
    base = add_products(
        here,
        None,
        (index, low, down),
        ((0, own[1]), (1, near[1]), (2, far[1]), (2, end_across[1])),
        weight,
        cut,
        tokens,
    )
    base, end_far[1], result = together(base, end_far[1], result)
    result = add_products(
        here, result, base, ((3, across[1]), (3, end_far[1])), weight, cut, tokens
    )
    result, end_far[2] = together(result, end_far[2])
    result = add_products(
        here, result, base, ((3, across[1]), (3, end_far[2])), weight, cut + tail, tokens, tail
    )
    grad_a = grad_a.reshape(-1, rank, attention_columns)
    grad_b = grad_b.reshape(-1, rank, columns)
    return result, grad_a, grad_b


def per_device(*arrays):
    sizes = tuple(lax.axis_size(a) for a in ("parts", "tensor", "dp"))
    tokens, attention_columns = arrays[0].shape
    columns = arrays[1].shape[1]
    fits = tokens % 1024 == 0 and attention_columns % 2048 == 0 and columns % 128 == 0
    if sizes == (2, 4, 4) and fits:
        return line_device(*arrays)
    return general_device(*arrays)


def solution(mesh):
    placed = (
        P(("parts", "dp"), "tensor"),
        P(("parts", "dp"), "tensor"),
        P(("parts", "dp")),
        P(),
        P("tensor", None),
        P(None, None, "tensor"),
        P(None, None, "tensor"),
    )
    return jax.shard_map(
        per_device,
        mesh=mesh,
        in_specs=placed,
        out_specs=(
            P(("parts", "dp"), "tensor"),
            P(("parts", "dp"), None, "tensor"),
            P(("parts", "dp"), None, "tensor"),
        ),
        check_vma=False,
    )
```

```python
import functools

import jax
import jax.numpy as jnp
from jax import lax
from jax.experimental import pallas as pl
from jax.experimental.pallas import tpu as pltpu
from jax.sharding import PartitionSpec as P

ADAPTER_SCALE = 2.0
OBJECTIVE_WEIGHT = 0.05
LAST_ROWS = 256
PIECE = 192
FIRST_EIGHTHS = 3

TO_ENDS = [(1, 0), (2, 3)]
MIDDLES = [(1, 2), (2, 1)]
FLIP_X, FLIP_CORE = 2, 1
LAST = (((1,), (1,)), ((), ()))
FIRST = (((0,), (0,)), ((), ()))
PLAIN = (((1,), (0,)), ((), ()))


def pairs(size, distance):
    return [(i, i ^ distance) for i in range(size)]


def power_of_two(size):
    return size & (size - 1) == 0


def low_rank_part(rows, values, chosen):
    adapters, tokens = chosen.shape
    terms = lax.dot_general(
        rows, values, (((1,), (1,)), ((), ())), preferred_element_type=jnp.float32
    )
    terms = terms.reshape(adapters, -1, tokens)
    return jnp.sum(jnp.where(chosen[:, None, :], terms, jnp.zeros((), jnp.float32)), axis=0)


def spread(chosen, low):
    adapters, tokens = chosen.shape
    wide = jnp.where(chosen[:, None, :], low[None], jnp.zeros((), low.dtype))
    return wide.reshape(adapters * low.shape[0], tokens)


def sum_over_tensor(part, size):
    if not power_of_two(size) or size > 4:
        return lax.psum(part, "tensor")
    terms = [part] + [lax.ppermute(part, "tensor", pairs(size, d)) for d in range(1, size)]
    while len(terms) > 1:
        terms = [terms[i] + terms[i + 1] for i in range(0, len(terms), 2)]
    return terms[0]


def reduce_to_owner(term_a, term_b, size):
    if size != 4:
        return tuple(
            lax.psum_scatter(t, "dp", scatter_dimension=0, tiled=True) for t in (term_a, term_b)
        )
    for distance in (1, 2):
        half = term_a.shape[0] // 2
        got_a = lax.ppermute(term_a[:half], "dp", pairs(size, distance))
        got_b = lax.ppermute(term_b[:half], "dp", pairs(size, distance))
        term_a = term_a[half:] + got_a
        term_b = term_b[half:] + got_b
    return term_a, term_b


def general_device(
    attention_output,
    projection_output_gradient,
    token_adapter_index,
    owner_slot_adapter,
    output_projection_weight,
    adapter_down_weight,
    adapter_up_weight,
):
    adapters, rank, attention_columns = adapter_down_weight.shape
    width_columns = adapter_up_weight.shape[2]
    tokens = attention_output.shape[0]
    tensor_size = lax.axis_size("tensor")
    dp_size = lax.axis_size("dp")
    input_rows = adapter_down_weight.reshape(adapters * rank, attention_columns)
    output_rows = adapter_up_weight.reshape(adapters * rank, width_columns)
    labels = jnp.arange(adapters, dtype=jnp.int32)
    chosen = labels[:, None] == token_adapter_index[None, :]
    row_dims = (((1,), (1,)), ((), ()))

    full_gradient = lax.all_gather(projection_output_gradient, "tensor", axis=1, tiled=True)

    out_part = low_rank_part(output_rows, projection_output_gradient, chosen)
    in_part = low_rank_part(input_rows, attention_output, chosen)
    low = sum_over_tensor(jnp.concatenate([in_part, out_part], axis=0), tensor_size)
    low_b = low.astype(jnp.bfloat16)
    in_b, out_b = low_b[:rank], low_b[rank:]

    if dp_size == 4:
        order = jnp.array([3, 1, 2, 0], jnp.int32) ^ lax.axis_index("dp")
        slots = owner_slot_adapter.reshape(dp_size, -1)[order].reshape(-1)
    else:
        slots = owner_slot_adapter
    owned = slots[:, None] == token_adapter_index[None, :]
    multiplier = ADAPTER_SCALE * OBJECTIVE_WEIGHT
    term_a = multiplier * jnp.dot(
        spread(owned, out_b), attention_output, preferred_element_type=jnp.float32
    )
    term_b = multiplier * jnp.dot(
        spread(owned, in_b), projection_output_gradient, preferred_element_type=jnp.float32
    )
    grad_a, grad_b = reduce_to_owner(term_a, term_b, dp_size)
    grad_a = grad_a.reshape(-1, rank, attention_columns)
    grad_b = grad_b.reshape(-1, rank, width_columns)

    wide = spread(chosen, out_b)
    contribution = lax.dot_general(
        wide, input_rows, (((0,), (0,)), ((), ())), preferred_element_type=jnp.float32
    )
    frozen = lax.dot_general(
        full_gradient, output_projection_weight, row_dims, preferred_element_type=jnp.float32
    )
    attention_gradient = (frozen + ADAPTER_SCALE * contribution).astype(jnp.bfloat16)
    return attention_gradient, grad_a, grad_b


def dot(a, b, dims):
    return lax.dot_general(a, b, dims, preferred_element_type=jnp.float32)


def kernel_call(body, **kwargs):
    return pl.pallas_call(
        body,
        compiler_params=pltpu.CompilerParams(vmem_limit_bytes=62 << 20),
        cost_estimate=pl.CostEstimate(flops=1 << 20, bytes_accessed=1 << 16, transcendentals=0),
        **kwargs,
    )


def together(*arrays):
    return lax.optimization_barrier(arrays)


def whole(array):
    return pl.BlockSpec(array.shape, lambda i, *_: (0,) * array.ndim)


def low_rank_kernel(rank, _, index_ref, down_ref, values_ref, up_ref, gradient_ref, out_ref):
    rows, tokens = down_ref.shape[0], values_ref.shape[0]
    step = pl.program_id(0)

    @pl.when(step == 0)
    def _():
        out_ref[...] = jnp.zeros_like(out_ref)

    adapter = lax.broadcasted_iota(jnp.int32, (rows // rank, 1, tokens), 0) + step * (rows // rank)
    chosen = adapter == index_ref[...][None]
    for at, weight, values in ((0, down_ref, values_ref), (rank, up_ref, gradient_ref)):
        terms = dot(weight[...], values[...], LAST).reshape(rows // rank, rank, tokens)
        out_ref[at : at + rank] += jnp.sum(jnp.where(chosen, terms, 0.0), axis=0)


def low_rank(after, index, down, values, up, gradient, rank):
    tokens = values.shape[0]
    rows = down.shape[0]
    block = rows // 4
    return kernel_call(
        functools.partial(low_rank_kernel, rank),
        grid=(4,),
        in_specs=[
            pl.BlockSpec(memory_space=pl.ANY),
            whole(index),
            pl.BlockSpec((block, down.shape[1]), lambda i: (i, 0)),
            whole(values),
            pl.BlockSpec((block, up.shape[1]), lambda i: (i, 0)),
            whole(gradient),
        ],
        out_specs=pl.BlockSpec((2 * rank, tokens), lambda i: (0, 0)),
        out_shape=jax.ShapeDtypeStruct((2 * rank, tokens), jnp.float32),
    )(after, index, down, values, up, gradient)


def spread_rows(labels, index, low):
    wide = jnp.concatenate([low] * (labels.shape[0] // low.shape[0]), axis=0)
    return jnp.where(labels == index, wide, 0.0).astype(jnp.bfloat16)


def adapter_gradient_kernel(
    here_ref, slots_ref, index_ref, pair, crossed, from_middle, values_ref, gradient_ref, send_ref, keep_ref, low_ref
):
    step = pl.program_id(0)

    @pl.when(step == 0)
    def _():
        middle = (here_ref[0] == 1) | (here_ref[0] == 2)
        total = pair[...] + crossed[...]
        low_ref[...] = jnp.where(middle, total, from_middle[...])

    rank = low_ref.shape[0] // 2
    low = low_ref[...].astype(jnp.bfloat16).astype(jnp.float32)
    multiplier = ADAPTER_SCALE * OBJECTIVE_WEIGHT
    a = multiplier * dot(
        spread_rows(slots_ref[...], index_ref[...], low[rank:]), values_ref[...], PLAIN
    )
    b = multiplier * dot(
        spread_rows(slots_ref[...], index_ref[...], low[:rank]), gradient_ref[...], PLAIN
    )
    split = a.shape[1]

    @pl.when(step < 2)
    def _():
        send_ref[:, :split] = a
        send_ref[:, split:] = b

    @pl.when(step >= 2)
    def _():
        keep_ref[:, :split] = a
        keep_ref[:, split:] = b


def adapter_gradients(here, slots, index, low_terms, values, gradient):
    rows = slots.shape[0]
    block = rows // 4
    width = values.shape[1] + gradient.shape[1]
    half = jax.ShapeDtypeStruct((rows // 2, width), jnp.float32)
    low = jax.ShapeDtypeStruct(low_terms[0].shape, jnp.float32)
    return kernel_call(
        adapter_gradient_kernel,
        grid_spec=pltpu.PrefetchScalarGridSpec(
            num_scalar_prefetch=1,
            grid=(4,),
            in_specs=[
                pl.BlockSpec((block, 1), lambda i, _: (i, 0)),
                whole(index),
                *(whole(term) for term in low_terms),
                whole(values),
                whole(gradient),
            ],
            out_specs=[
                pl.BlockSpec((block, width), lambda i, _: (jnp.minimum(i, 1), 0)),
                pl.BlockSpec((block, width), lambda i, _: (jnp.maximum(i - 2, 0), 0)),
                whole(low),
            ],
        ),
        out_shape=[half, half, low],
    )(here, slots, index, *low_terms, values, gradient)


def halves_kernel(keep_ref, got_ref, send_ref, out_ref):
    total = keep_ref[...] + got_ref[...]

    @pl.when(pl.program_id(0) < 2)
    def _():
        send_ref[...] = total.astype(send_ref.dtype)

    @pl.when(pl.program_id(0) >= 2)
    def _():
        out_ref[...] = total


def add_in_halves(keep, got):
    rows, width = keep.shape
    block = rows // 4
    both = pl.BlockSpec((block, width), lambda i: (i, 0))
    return kernel_call(
        halves_kernel,
        grid=(4,),
        in_specs=[both, both],
        out_specs=[
            pl.BlockSpec((block, width), lambda i: (jnp.minimum(i, 1), 0)),
            pl.BlockSpec((block, width), lambda i: (jnp.maximum(i - 2, 0), 0)),
        ],
        out_shape=[
            jax.ShapeDtypeStruct((rows // 2, width), jnp.bfloat16),
            jax.ShapeDtypeStruct((rows // 2, width), jnp.float32),
        ],
    )(keep, got)


def owned_kernel(keep_ref, got_ref, a_ref, b_ref):
    split = a_ref.shape[1]
    a_ref[...] = keep_ref[:, :split] + got_ref[:, :split].astype(jnp.float32)
    b_ref[...] = keep_ref[:, split:] + got_ref[:, split:].astype(jnp.float32)


def owned_sums(keep, got, split):
    rows, width = keep.shape
    block = rows // 4
    widths = (split, width - split)
    return kernel_call(
        owned_kernel,
        grid=(4,),
        in_specs=[pl.BlockSpec((block, width), lambda i: (i, 0))] * 2,
        out_specs=[pl.BlockSpec((block, w), lambda i: (i, 0)) for w in widths],
        out_shape=[jax.ShapeDtypeStruct((rows, w), jnp.float32) for w in widths],
    )(keep, got)


def rows_kernel(distances, first, here_ref, _, *refs):
    with_adapters = first is not None
    start_count = 3 if with_adapters else 1
    start_refs, refs = refs[:start_count], refs[start_count:]
    arrays, (weight_ref, out_ref, *scratch) = refs[: len(distances)], refs[len(distances) :]
    if with_adapters:
        index_ref, low_ref, rows_ref = start_refs
        (wide_ref,) = scratch

        @pl.when(pl.program_id(0) == 0)
        def _():
            rank = low_ref.shape[0] // 2
            labels = lax.broadcasted_iota(jnp.int32, wide_ref.shape[::-1], 0) // rank
            here_tokens = pl.ds(first, wide_ref.shape[0])
            low = low_ref[rank:, here_tokens].astype(jnp.bfloat16).astype(jnp.float32)
            wide_ref[...] = spread_rows(labels, index_ref[:, here_tokens], low).T

        total = ADAPTER_SCALE * dot(wide_ref[...], rows_ref[...], PLAIN)
    else:
        total = start_refs[0][...]
    columns = arrays[0].shape[1]
    blocks = {}
    for distance, ref in zip(distances, arrays):
        blocks[distance] = blocks[distance] + ref[...] if distance in blocks else ref[...]
    for distance, block in blocks.items():
        if weight_ref.shape[1] == columns:
            total += dot(block, weight_ref[...], LAST)
        else:
            at = pl.multiple_of((here_ref[0] ^ distance) * columns, 128)
            total += dot(block, weight_ref[:, pl.ds(at, columns)], LAST)
    out_ref[...] = total.astype(out_ref.dtype)


def add_products(here, before, start, blocks, weight, first, tokens, skip=0):
    step = blocks[-1][1].shape[0]
    features, width = weight.shape
    block = 1024 if len(blocks) == 2 else 512
    if before is None:
        out = jax.ShapeDtypeStruct((step, features), jnp.float32)
        out_block = pl.BlockSpec((step, block), lambda i, _: (0, i))
    elif first == 0:
        out = jax.ShapeDtypeStruct((tokens, features), jnp.bfloat16)
        out_block = pl.BlockSpec((step, block), lambda i, _: (0, i))
    else:
        out = jax.ShapeDtypeStruct((tokens, features), jnp.bfloat16)
        out_block = pl.BlockSpec(
            (pl.Element(step), pl.Element(block)), lambda i, _: (first, i * block)
        )
    distances, arrays = zip(*blocks)
    if len(set(distances)) == 1:
        weight_block = pl.BlockSpec(
            (block, arrays[0].shape[1]), lambda i, here: (i, here[0] ^ distances[0])
        )
    else:
        weight_block = pl.BlockSpec((block, width), lambda i, _: (i, 0))
    with_adapters = isinstance(start, tuple)
    if with_adapters:
        index, low, rows = start
        start_blocks = [
            whole(index),
            whole(low),
            pl.BlockSpec((rows.shape[0], block), lambda i, _: (0, i)),
        ]
        scratch = [pltpu.VMEM((step, rows.shape[0]), jnp.bfloat16)]
    else:
        start = (start,)
        start_blocks = [
            pl.BlockSpec((pl.Element(step), pl.Element(block)), lambda i, _: (skip, i * block))
        ]
        scratch = []
    return kernel_call(
        functools.partial(rows_kernel, distances, first if with_adapters else None),
        grid_spec=pltpu.PrefetchScalarGridSpec(
            num_scalar_prefetch=1,
            grid=(features // block,),
            in_specs=[
                pl.BlockSpec(memory_space=pl.ANY),
                *start_blocks,
                *(
                    pl.BlockSpec(
                        (pl.Element(step), pl.Element(b.shape[1])),
                        lambda i, _, b=b: (skip if b.shape[0] > step else 0, 0),
                    )
                    for b in arrays
                ),
                weight_block,
            ],
            out_specs=out_block,
            scratch_shapes=scratch,
        ),
        out_shape=out,
        input_output_aliases={} if before is None or before is here else {1: 0},
    )(here, here if before is None else before, *start, *arrays, weight)


def line_device(
    attention_output,
    projection_output_gradient,
    token_adapter_index,
    owner_slot_adapter,
    output_projection_weight,
    adapter_down_weight,
    adapter_up_weight,
):
    adapters, rank, attention_columns = adapter_down_weight.shape
    columns = adapter_up_weight.shape[2]
    tokens = attention_output.shape[0]
    here = lax.axis_index("tensor")[None]
    down = adapter_down_weight.reshape(adapters * rank, attention_columns)
    up = adapter_up_weight.reshape(adapters * rank, columns)
    index = token_adapter_index[None, :]

    cut = tokens * FIRST_EIGHTHS // 8
    order = jnp.array([3, 1, 2, 0], jnp.int32) ^ lax.axis_index("dp")
    slots = jnp.repeat(owner_slot_adapter.reshape(4, -1)[order].reshape(-1), rank)[:, None]
    weight = output_projection_weight

    def swap(block):
        return lax.ppermute(block, "tensor", pairs(4, 1))

    def cross(block):
        return lax.ppermute(block, "tensor", MIDDLES)

    def to_end(block):
        return lax.ppermute(block, "tensor", TO_ENDS)

    own = [projection_output_gradient[:cut], projection_output_gradient[cut:]]
    near, across, far, end_across, end_far = ({} for _ in range(5))

    near[0], across[0] = swap(own[0]), cross(own[0])
    low_part = low_rank(index, index, down, attention_output, up, projection_output_gradient, rank)
    low_near = swap(low_part)
    own_first, own_rest = own[1][:PIECE], own[1][PIECE:]
    near[0], across[0], low_near, own_first = together(near[0], across[0], low_near, own_first)
    near_first = swap(own_first)
    pair = low_part + low_near
    crossed = cross(pair)
    pair, crossed, near[0] = together(pair, crossed, near[0])
    from_middle = to_end(pair + crossed)
    near_first, from_middle, own_rest, near[0] = together(
        near_first, from_middle, own_rest, near[0]
    )
    near_rest, far[0] = swap(own_rest), cross(near[0])
    low_terms = (pair, crossed, from_middle)
    send, keep, low = adapter_gradients(
        here, slots, index, low_terms, attention_output, projection_output_gradient
    )
    send, keep, near_rest, far[0], across[0], own[1], index = together(
        send, keep, near_rest, far[0], across[0], own[1], index
    )
    end_across[0], across[1] = to_end(across[0]), cross(own[1])
    got = lax.ppermute(send, "dp", pairs(4, FLIP_CORE))
    end_far[0] = to_end(far[0])
    got, near_first, near_rest = together(got, near_first, near_rest)
    near[1] = jnp.concatenate([near_first, near_rest], axis=0)
    far[1] = cross(near[1])
    to_x, keep = add_in_halves(keep, got)
    to_x, keep, end_across[0], across[1], index = together(
        to_x, keep, end_across[0], across[1], index
    )
    got = lax.ppermute(to_x, "dp", pairs(4, FLIP_X))
    end_across[1] = to_end(across[1])
    base0 = add_products(
        here,
        None,
        (index, low, down),
        ((0, own[0]), (1, near[0]), (2, far[0]), (2, end_across[0])),
        weight,
        0,
        tokens,
    )
    base0, end_far[0] = together(base0, end_far[0])
    result = add_products(
        here, here, base0, ((3, across[0]), (3, end_far[0])), weight, 0, tokens
    )
    result, far[1], index = together(result, far[1], index)
    tail = far[1].shape[0] - LAST_ROWS
    end_far[1], end_far[2] = to_end(far[1][:tail]), to_end(far[1][tail:])
    grad_a, grad_b = owned_sums(keep, got, attention_columns)
    grad_a, grad_b, end_across[1], index = together(grad_a, grad_b, end_across[1], index)
    base = add_products(
        here,
        None,
        (index, low, down),
        ((0, own[1]), (1, near[1]), (2, far[1]), (2, end_across[1])),
        weight,
        cut,
        tokens,
    )
    base, end_far[1], result = together(base, end_far[1], result)
    result = add_products(
        here, result, base, ((3, across[1]), (3, end_far[1])), weight, cut, tokens
    )
    result, end_far[2] = together(result, end_far[2])
    result = add_products(
        here, result, base, ((3, across[1]), (3, end_far[2])), weight, cut + tail, tokens, tail
    )
    grad_a = grad_a.reshape(-1, rank, attention_columns)
    grad_b = grad_b.reshape(-1, rank, columns)
    return result, grad_a, grad_b


def per_device(*arrays):
    sizes = tuple(lax.axis_size(a) for a in ("parts", "tensor", "dp"))
    tokens, attention_columns = arrays[0].shape
    columns = arrays[1].shape[1]
    fits = tokens % 1024 == 0 and attention_columns % 2048 == 0 and columns % 128 == 0
    if sizes == (2, 4, 4) and fits:
        return line_device(*arrays)
    return general_device(*arrays)


def solution(mesh):
    placed = (
        P(("parts", "dp"), "tensor"),
        P(("parts", "dp"), "tensor"),
        P(("parts", "dp")),
        P(),
        P("tensor", None),
        P(None, None, "tensor"),
        P(None, None, "tensor"),
    )
    return jax.shard_map(
        per_device,
        mesh=mesh,
        in_specs=placed,
        out_specs=(
            P(("parts", "dp"), "tensor"),
            P(("parts", "dp"), None, "tensor"),
            P(("parts", "dp"), None, "tensor"),
        ),
        check_vma=False,
    )
```
